32 devices in a mesh: rep: 8 (over y, x, core), shard: 4 (over z).
Axes of the slice: x: 2, y: 2, z: 4, core: 2. Of those that a mesh axis runs over, the one named last changes fastest.
Arguments:
- x_in: bfloat16 [32, 1024, 1024], P(('rep', 'shard')), may hold values from -6 to 6
- segment_ids: int32 [32, 1024], P(('rep', 'shard')), may hold values from 0 to 3, never falling along the last dimension, each value on 1 to 512 neighbouring positions
- norm_in: bfloat16 [1024], P('shard'), may hold values from 0.5 to 1.5
- mix_in: bfloat16 [1024, 3352], P('shard'), may hold values from -0.1875 to 0.1875
- attn_in: bfloat16 [1024, 768], P('shard'), may hold values from -0.1875 to 0.1875
- attn_out: bfloat16 [1024, 512], P('shard'), may hold values from -0.75 to 0.75
- mix_out: bfloat16 [1024, 1536], P('shard'), may hold values from -0.15625 to 0.15625
- norm_ff: bfloat16 [1024], P('shard'), may hold values from 0.5 to 1.5
- ff_in: bfloat16 [1024, 4096], P('shard'), may hold values from -0.1875 to 0.1875
- ff_out: bfloat16 [1024, 2048], P('shard'), may hold values from -0.125 to 0.125
- conv_kernel: bfloat16 [4, 1792], replicated, may hold values from -3 to 3
- conv_bias: bfloat16 [1792], replicated, may hold values from -3 to 3
- log_rate: float32 [24], replicated, may hold values from 0 to 2.77
- dt_bias: float32 [24], replicated, may hold values from -4.6 to -2.3
- skip: float32 [24], replicated, may hold values from 0.5 to 1.5
- gate_norm: bfloat16 [1536], replicated, may hold values from 0.5 to 1.5
- cotangent: bfloat16 [32, 1024, 1024], P(('rep', 'shard')), may hold values from -6 to 6
Outputs:
- output: bfloat16 [32, 1024, 1024], P(('rep', 'shard'))
- input_grad: bfloat16 [32, 1024, 1024], P(('rep', 'shard'))
- norm_in_grad: float32 [1024], P('shard')
- mix_in_grad: float32 [1024, 3352], P('shard')
- attn_in_grad: float32 [1024, 768], P('shard')
- attn_out_grad: float32 [1024, 512], P('shard')
- mix_out_grad: float32 [1024, 1536], P('shard')
- norm_ff_grad: float32 [1024], P('shard')
- ff_in_grad: float32 [1024, 4096], P('shard')
- ff_out_grad: float32 [1024, 2048], P('shard')
- conv_kernel_grad: float32 [4, 1792], replicated
- conv_bias_grad: float32 [1792], replicated
- log_rate_grad: float32 [24], replicated
- dt_bias_grad: float32 [24], replicated
- skip_grad: float32 [24], replicated
- gate_norm_grad: float32 [1536], replicated
The draws below stay inside these ranges and needn't reach their ends.
Inputs may be any that keep to these rules, and one draw needn't show every extreme that they name: `segment_ids`: within a sequence segment numbers never fall, so each document is one run of tokens; every number of 0 to 3 occurs in each sequence, in runs of at most 512 tokens.
All inputs are finite; a program needn't handle non-finite values.
Results may differ from the reference program's by a relative error of at most 0.019.
Values may be sent and summed in bfloat16 or wider, within the bound.
No kernel may reach another device: no remote copies, remote signals or barrier semaphores. Data moves between devices by JAX's collectives and lax.ppermute only.
A program may use at most 320 MiB of HBM per device.

```python
import math
import jax
import jax.numpy as jnp
import numpy as np
from jax import lax

D = 1024
FF = 2048
AHEADS = 8
KVHEADS = 2
HDIM = 64
MHEADS = 24
CONV = 4
SEQ_LEN = 1024
SEQS = 32
DSSM = 1536
XBC = 1792
INPROJ = 3352
ATTW = 512
QKV = 768


def level_of(stream_key, extent, shards, smallest, high):
    level = 1.0
    for position, blocks in shards:
        heights = jax.random.uniform(jax.random.fold_in(jax.random.fold_in(stream_key, 6), position), (blocks,), jnp.float32, smallest / len(shards), high / len(shards))
        level = level * jnp.repeat(jnp.exp(heights), extent[position] // blocks).reshape((-1,) + (1,) * (len(extent) - 1 - position))
    return level


def length_profile(count, total, bound, skew):
    portions = [(1 << 20) // math.isqrt(grade ** skew) + 1 for grade in range(2, count + 1)]
    spare, counts = total - bound - (count - 1), [1] * (count - 1)
    while spare > 0:
        movable = [i for i in range(count - 1) if counts[i] < bound]
        pool, budget = sum([portions[i] for i in movable]), spare
        for i in movable:
            more = min(bound - counts[i], max(1, budget * portions[i] // pool), spare)
            counts[i] = counts[i] + more
            spare = spare - more
    return np.array([bound] + counts)


def uneven(rng, amount, total, bound, skew):
    if amount == 2:
        one = jax.random.randint(rng, (), max(1, total - bound), min(bound, total - 1) + 1)
        return jnp.stack([one, total - one])
    lengths = jnp.asarray(length_profile(amount, total, bound, skew), jnp.int32)
    pairs = (amount - 1) // 2
    giver, receiver = lengths[1:1 + 2 * pairs:2], lengths[2:2 + 2 * pairs:2]
    room = jnp.minimum(giver - 1, bound - receiver)
    shifted = jax.random.randint(jax.random.fold_in(rng, 1), (pairs,), 0, 1 << 20) % (room + 1)
    lengths = lengths.at[1:1 + 2 * pairs:2].set(giver - shifted).at[2:2 + 2 * pairs:2].set(receiver + shifted)
    return lengths[jax.random.permutation(jax.random.fold_in(rng, 2), amount)]


def centred(own_key, extent, scale, most, pieces=(), kind=jnp.bfloat16):
    level = level_of(own_key, extent, pieces, -0.22, 0.18) if pieces else 1.0
    drawn = jax.random.normal(own_key, extent, jnp.float32) * scale * level
    return jnp.minimum(jnp.maximum(drawn, -most), most).astype(kind)


def setup_inputs(seed: int = 0) -> dict:
    seeds = jax.random.split(jax.random.key(seed), 18)
    x_in = centred(seeds[0], (SEQS, SEQ_LEN, D), 1.0, 6.0, ((0, 32),))
    segment_ids = jax.vmap(lambda own: jnp.searchsorted(jnp.cumsum(uneven(own, 4, SEQ_LEN, SEQ_LEN // 2, 1)), jnp.arange(SEQ_LEN), side="right"))(jax.random.split(seeds[1], SEQS)).reshape((SEQS, SEQ_LEN)).astype(jnp.int32)
    norm_in = jnp.clip(1.0 + 0.1 * jax.random.normal(seeds[2], (D,), jnp.float32), 0.5, 1.5).astype(jnp.bfloat16)
    mix_in = centred(seeds[3], (D, INPROJ), D ** -0.5, 0.1875, ((0, 4),))
    attn_in = centred(seeds[4], (D, QKV), D ** -0.5, 0.1875, ((0, 4),))
    attn_out = centred(seeds[5], (D, ATTW), (ATTW // 8) ** -0.5, 0.75, ((0, 4),))
    mix_out = centred(seeds[6], (D, DSSM), DSSM ** -0.5, 0.15625, ((0, 4),))
    norm_ff = jnp.clip(1.0 + 0.1 * jax.random.normal(seeds[7], (D,), jnp.float32), 0.5, 1.5).astype(jnp.bfloat16)
    ff_in = centred(seeds[8], (D, 2 * FF), D ** -0.5, 0.1875, ((0, 4),))
    ff_out = centred(seeds[9], (D, FF), FF ** -0.5, 0.125, ((0, 4),))
    conv_kernel = centred(seeds[10], (CONV, XBC), CONV ** -0.5, 3.0)
    conv_bias = centred(seeds[11], (XBC,), 0.5, 3.0)
    log_rate = jnp.clip(jax.random.uniform(seeds[12], (MHEADS,), jnp.float32, 0.0, 2.77), 0.0, 2.77)
    dt_bias = jnp.clip(jax.random.uniform(seeds[13], (MHEADS,), jnp.float32, -4.6, -2.3), -4.6, -2.3)
    skip = jnp.clip(jax.random.uniform(seeds[14], (MHEADS,), jnp.float32, 0.5, 1.5), 0.5, 1.5)
    gate_norm = jnp.clip(1.0 + 0.1 * jax.random.normal(seeds[15], (DSSM,), jnp.float32), 0.5, 1.5).astype(jnp.bfloat16)
    cotangent = centred(seeds[16], (SEQS, SEQ_LEN, D), 1.0, 6.0, ((0, 32),))
    return {"x_in": x_in, "segment_ids": segment_ids, "norm_in": norm_in, "mix_in": mix_in, "attn_in": attn_in, "attn_out": attn_out, "mix_out": mix_out, "norm_ff": norm_ff, "ff_in": ff_in, "ff_out": ff_out, "conv_kernel": conv_kernel, "conv_bias": conv_bias, "log_rate": log_rate, "dt_bias": dt_bias, "skip": skip, "gate_norm": gate_norm, "cotangent": cotangent}


EPS = 1e-05
THETA = 100000000000.0
HIGH = lax.Precision.HIGHEST

@jax.custom_vjp
def low(v):
    return lax.optimization_barrier(v.astype(jnp.bfloat16)).astype(jnp.float32)

@jax.custom_vjp
def low_back(v):
    return v

def low_keep(v):
    return (low(v), None)

def low_pass(kept, grad):
    return (grad,)

def back_keep(v):
    return (v, None)

def back_low(kept, grad):
    return (low(grad),)
low.defvjp(low_keep, low_pass)
low_back.defvjp(back_keep, back_low)

def both_ways(values):
    return low(low_back(values))

def hdot(left, right):
    return jnp.dot(left, right, precision=HIGH, preferred_element_type=jnp.float32)

def hdot_nt(left, right):
    return jnp.dot(left, right.T, precision=HIGH, preferred_element_type=jnp.float32)

def normed(values, gain):
    scale = lax.rsqrt(lax.optimization_barrier(jnp.mean(values * values, axis=-1, keepdims=True)) + EPS)
    return values * scale * gain

def swiglu(projection):
    width = projection.shape[-1] // 2
    return jax.nn.silu(projection[:, :width]) * projection[:, width:]

def rotary_tables(length, width):
    half = width // 2
    freq = jnp.exp(-(jnp.arange(half, dtype=jnp.float32) * (2.0 / width)) * math.log(THETA))
    angle = jnp.arange(length, dtype=jnp.float32)[:, None] * freq[None, :]
    return (jnp.cos(angle), jnp.sin(angle))

def rotate(values, cosine, sine):
    half = values.shape[-1] // 2
    first = values[..., :half]
    second = values[..., half:]
    cos_b = cosine[None, :, None, :]
    sin_b = sine[None, :, None, :]
    return jnp.concatenate([first * cos_b - second * sin_b, second * cos_b + first * sin_b], axis=-1)

def attention_inputs(attn_proj, cosine, sine):
    sequences, length = (attn_proj.shape[0], attn_proj.shape[1])
    width = AHEADS * HDIM
    query = rotate(attn_proj[..., :width].reshape(sequences, length, AHEADS, HDIM), cosine, sine)
    keys = rotate(attn_proj[..., width:width + KVHEADS * HDIM].reshape(sequences, length, KVHEADS, HDIM), cosine, sine)
    values = attn_proj[..., width + KVHEADS * HDIM:].reshape(sequences, length, KVHEADS, HDIM)
    return (query, keys, values)

def conv_mixed(conv_input, segment_ids, conv_kernel, conv_bias):
    length = conv_input.shape[1]
    total = conv_bias + conv_kernel[CONV - 1] * conv_input
    for offset in range(1, CONV):
        earlier = jnp.pad(conv_input, ((0, 0), (offset, 0), (0, 0)))[:, :length]
        earlier_ids = jnp.pad(segment_ids, ((0, 0), (offset, 0)), constant_values=-1)[:, :length]
        total = total + conv_kernel[CONV - 1 - offset] * jnp.where((earlier_ids == segment_ids)[..., None], earlier, 0.0)
    return jax.nn.silu(total)

def scan_block(carry, item):
    state, last_id = carry
    inputs, step_sizes, log_decay, b_values, c_values, block_ids = item
    block = block_ids.shape[0]
    order = jnp.arange(block, dtype=jnp.int32)
    same = (block_ids[:, None] == block_ids[None, :]) & (order[:, None] >= order[None, :])
    totals = jnp.cumsum(log_decay, axis=0).T
    gaps = totals[:, :, None] - totals[:, None, :]
    decays = jnp.where(same[None], jnp.exp(jnp.where(same[None], gaps, 0.0)), 0.0)
    intersection = jnp.dot(c_values, b_values.T, precision=HIGH, preferred_element_type=jnp.float32)
    mixing = decays * intersection[None] * step_sizes.T[:, None, :]
    within = jnp.einsum('hts,shp->thp', mixing, inputs, precision=HIGH)
    entering = jnp.where((block_ids == last_id)[:, None], jnp.exp(totals.T), 0.0)
    carried = jnp.einsum('tn,hpn->thp', c_values, state, precision=HIGH) * entering[:, :, None]
    tail_id = block_ids[block - 1]
    leaving = jnp.where((block_ids == tail_id)[:, None], jnp.exp(totals[:, block - 1:] - totals).T, 0.0)
    kept_rate = jnp.where(tail_id == last_id, jnp.exp(totals[:, block - 1]), 0.0)
    fresh = jnp.einsum('shp,sn->hpn', inputs * (leaving * step_sizes)[:, :, None], b_values, precision=HIGH)
    return ((fresh + state * kept_rate[:, None, None], tail_id), within + carried)

def ssd_sequence(inputs, step_sizes, rate, b_values, c_values, segment_ids):
    length, heads, width = inputs.shape
    block = min(128, length)
    blocks = length // block
    log_decay = step_sizes * rate[None, :]

    def cut(values):
        return values.reshape((blocks, block) + values.shape[1:])
    initial = (jnp.zeros((heads, width, b_values.shape[1]), jnp.float32), jnp.array(-1, jnp.int32))
    final, outputs = lax.scan(jax.checkpoint(scan_block), initial, (cut(inputs), cut(step_sizes), cut(log_decay), cut(b_values), cut(c_values), cut(segment_ids)))
    return outputs.reshape(length, heads, width)

def mixer_core(projected, segment_ids, conv_kernel, conv_bias, log_rate, dt_bias, skip, gate_norm):
    inner = gate_norm.shape[0]
    heads = log_rate.shape[0]
    width = inner // heads
    channels = conv_bias.shape[0]
    states = (channels - inner) // 2
    sequences, length = segment_ids.shape
    gate_part = projected[..., :inner]
    conv_input = projected[..., inner:inner + channels]
    step_raw = projected[..., inner + channels:]
    conv_out = conv_mixed(conv_input, segment_ids, conv_kernel, conv_bias)
    inputs = conv_out[..., :inner].reshape(sequences, length, heads, width)
    b_values = conv_out[..., inner:inner + states]
    c_values = conv_out[..., inner + states:]
    step_sizes = jax.nn.softplus(step_raw + dt_bias)
    rate = -jnp.exp(log_rate)
    scanned = jax.vmap(ssd_sequence, in_axes=(0, 0, None, 0, 0, 0))(inputs, step_sizes, rate, b_values, c_values, segment_ids)
    output = scanned + skip[:, None] * inputs
    gated = output.reshape(sequences, length, inner) * jax.nn.silu(gate_part)
    return normed(gated, gate_norm)

def attend_exact(query, keys, values, query_ids, key_ids, query_pos):
    scale = query.shape[-1] ** (-0.5)
    scores = low_back(jnp.einsum('qkgd,skd->kgqs', query, keys, precision=HIGH) * scale)
    key_pos = jnp.arange(keys.shape[0], dtype=jnp.int32)
    allowed = (query_ids[:, None] == key_ids[None, :]) & (query_pos[:, None] >= key_pos[None, :])
    scores = jnp.where(allowed[None, None], scores, -jnp.inf)
    top = lax.optimization_barrier(jnp.max(scores, axis=-1, keepdims=True))
    expd = jnp.exp(scores - top)
    probs = expd / lax.optimization_barrier(jnp.sum(expd, axis=-1, keepdims=True))
    return jnp.einsum('kgqs,skd->qkgd', low(probs), values, precision=HIGH)

def attention_sequence(query, keys, values, segment_ids):
    length = query.shape[0]
    block = min(512, length)
    blocks = length // block
    positions = jnp.arange(length, dtype=jnp.int32)

    def one_block(index):
        start = index * block
        part = lax.dynamic_slice_in_dim(query, start, block, 0)
        part_ids = lax.dynamic_slice_in_dim(segment_ids, start, block, 0)
        part_pos = lax.dynamic_slice_in_dim(positions, start, block, 0)
        return attend_exact(part, keys, values, part_ids, segment_ids, part_pos)
    outputs = lax.map(jax.checkpoint(one_block), jnp.arange(blocks, dtype=jnp.int32))
    return outputs.reshape(query.shape)

def layer(resid, segment_ids, gain_in, mix_in, attn_in, attn_out, mix_out, gain_ff, ff_in, ff_out, conv_kernel, conv_bias, log_rate, dt_bias, skip, gate_norm):
    sequences, length, model = resid.shape
    tokens = sequences * length
    flat = resid.reshape(tokens, model)
    first_low = low(normed(flat, gain_in))
    projected = low_back(hdot(first_low, mix_in))
    attn_proj = low_back(hdot(first_low, attn_in))
    mixed_norm = mixer_core(projected.reshape(sequences, length, -1), segment_ids, conv_kernel, conv_bias, log_rate, dt_bias, skip, gate_norm)
    mixer_branch = low_back(hdot_nt(low(mixed_norm.reshape(tokens, -1)), mix_out))
    cosine, sine = rotary_tables(length, HDIM)
    query, keys, values = attention_inputs(attn_proj.reshape(sequences, length, -1), cosine, sine)
    groups = AHEADS // KVHEADS
    query = low(query).reshape(sequences, length, KVHEADS, groups, HDIM)
    keys = low(keys)
    values = low(values)
    attended = jax.vmap(attention_sequence)(query, keys, values, segment_ids)
    attended = both_ways(attended.reshape(tokens, -1))
    attn_branch = low_back(hdot_nt(attended, attn_out))
    hidden = flat + attn_branch + mixer_branch
    second_low = low(normed(hidden, gain_ff))
    ff_proj = low_back(hdot(second_low, ff_in))
    ff_branch = low_back(hdot_nt(low(swiglu(ff_proj)), ff_out))
    return (hidden + ff_branch).reshape(resid.shape)

def reference(x_in, segment_ids, norm_in, mix_in, attn_in, attn_out, mix_out, norm_ff, ff_in, ff_out, conv_kernel, conv_bias, log_rate, dt_bias, skip, gate_norm, cotangent):
    params = tuple((item.astype(jnp.float32) for item in (norm_in, mix_in, attn_in, attn_out, mix_out, norm_ff, ff_in, ff_out, conv_kernel, conv_bias, log_rate, dt_bias, skip, gate_norm)))
    total_seqs = x_in.shape[0]
    group = math.gcd(total_seqs, max(1, 4096 // x_in.shape[1]))
    groups_count = total_seqs // group

    def cut(values):
        return values.reshape((groups_count, group) + values.shape[1:])

    def one_group(sums, item):
        resid, group_ids, grad_out = item

        def apply(inputs, *weights):
            return layer(inputs, group_ids, *weights)
        output, back = jax.vjp(apply, resid.astype(jnp.float32), *params)
        grads = back(grad_out.astype(jnp.float32))
        new_sums = tuple((left + right for left, right in zip(sums, grads[1:])))
        return (new_sums, (output.astype(jnp.bfloat16), grads[0].astype(jnp.bfloat16)))
    zeros = tuple((jnp.zeros(item.shape, jnp.float32) for item in params))
    sums, (outputs, input_grads) = lax.scan(one_group, zeros, (cut(x_in), cut(segment_ids), cut(cotangent)))
    return (outputs.reshape(x_in.shape), input_grads.reshape(x_in.shape), sums[0], sums[1], sums[2], sums[3], sums[4], sums[5], sums[6], sums[7], sums[8], sums[9], sums[10], sums[11], sums[12], sums[13])
```

```python
from functools import partial
import math

import jax
import jax.numpy as jnp
from jax import lax
from jax.experimental import pallas as pl
from jax.experimental.pallas import tpu as pltpu
from jax.sharding import PartitionSpec as P

AHEADS = 8
KVHEADS = 2
HDIM = 64
CONV = 4
EPS = 1e-05
THETA = 100000000000.0
HIGH = lax.Precision.HIGHEST
F32 = jnp.float32
BF16 = jnp.bfloat16
LANES = 128
CHUNK = 128
QBLOCK = 256
LONGEST = 512


def dot_nn(left, right, precision=None):
    return lax.dot_general(
        left, right, (((1,), (0,)), ((), ())), precision=precision, preferred_element_type=F32
    )


def dot_nt(left, right):
    return lax.dot_general(left, right, (((1,), (1,)), ((), ())), preferred_element_type=F32)


def dot_tn(left, right):
    return lax.dot_general(left, right, (((0,), (0,)), ((), ())), preferred_element_type=F32)


def sigmoid(values):
    return 0.5 * jnp.tanh(0.5 * values) + 0.5


def softplus(values):
    return jnp.maximum(values, 0.0) + jnp.log1p(jnp.exp(-jnp.abs(values)))


def iota(shape, axis):
    return lax.broadcasted_iota(jnp.int32, shape, axis)


def split_low(values):
    high = values.astype(BF16)
    return high, (values - high.astype(F32)).astype(BF16)


def turn(values, cosine, sine, sign):
    lane = iota(values.shape, 1)
    partner = jnp.where(
        (lane % HDIM) < HDIM // 2,
        -pltpu.roll(values, LANES - HDIM // 2, 1),
        pltpu.roll(values, HDIM // 2, 1),
    )
    return values * cosine + sign * partner * sine


def twice(values, head, low_half):
    swapped = pltpu.roll(values, HDIM, 1)
    return jnp.where(low_half == (head == 0), values, swapped)


def attention_fwd_kernel(proj_ref, cos_ref, sin_ref, idc_ref, idr_ref, q_ref, k_ref, v_ref, out_ref, lse_ref, k2_ref, v2_ref):
    length = proj_ref.shape[0]
    pairs = AHEADS // 2
    cosine = cos_ref[...]
    sine = sin_ref[...]
    for slab in range(pairs):
        cols = slice(slab * LANES, (slab + 1) * LANES)
        q_ref[:, cols] = turn(proj_ref[:, cols], cosine, sine, 1.0).astype(BF16)
    at = pairs * LANES
    keys = turn(proj_ref[:, at : at + LANES], cosine, sine, 1.0)
    values = proj_ref[:, at + LANES : at + 2 * LANES]
    k_ref[...] = keys.astype(BF16)
    v_ref[...] = values.astype(BF16)
    low_half = iota((length, LANES), 1) < HDIM
    for head in range(KVHEADS):
        k2_ref[head] = twice(keys, head, low_half).astype(BF16)
        v2_ref[head] = twice(values, head, low_half).astype(BF16)
    scale = HDIM ** (-0.5)
    low_q = iota((QBLOCK, LANES), 1) < HDIM
    zero = jnp.zeros((QBLOCK, LANES), BF16)
    for block in range(length // QBLOCK):
        start, stop = block * QBLOCK, (block + 1) * QBLOCK
        first = max(0, start - LONGEST)
        window = stop - first
        key_pos = iota((window, QBLOCK), 0) + first
        query_pos = iota((window, QBLOCK), 1) + start
        allowed = (idc_ref[first:stop, :] == idr_ref[:, start:stop]) & (query_pos >= key_pos)
        bias = jnp.where(allowed, 0.0, -1e30)
        for pair in range(pairs):
            group = pair * 2 // (AHEADS // KVHEADS)
            cols = slice(pair * LANES, (pair + 1) * LANES)
            query = q_ref[start:stop, cols]
            k2 = k2_ref[group, first:stop, :]
            v2 = v2_ref[group, first:stop, :]
            outs = []
            for side in range(2):
                part = jnp.where(low_q, query, zero) if side == 0 else jnp.where(low_q, zero, query)
                scores = dot_nt(k2, part) * scale + bias
                top = jnp.max(scores, axis=0, keepdims=True)
                expd = jnp.exp(scores - top)
                total = jnp.sum(expd, axis=0, keepdims=True)
                probs = (expd * (1.0 / total)).astype(BF16)
                outs.append(dot_tn(probs, v2))
                lse_ref[2 * pair + side : 2 * pair + side + 1, start:stop] = top + jnp.log(total)
            out_ref[start:stop, cols] = jnp.where(low_q, outs[0], outs[1]).astype(BF16)


def attention_fwd(proj, cosine, sine, id_col, id_row):
    length = proj.shape[0]
    shape = jax.ShapeDtypeStruct
    return pl.pallas_call(
        attention_fwd_kernel,
        out_shape=(
            shape((length, AHEADS * HDIM), BF16),
            shape((length, LANES), BF16),
            shape((length, LANES), BF16),
            shape((length, AHEADS * HDIM), BF16),
            shape((AHEADS, length), F32),
        ),
        scratch_shapes=[
            pltpu.VMEM((KVHEADS, length, LANES), BF16),
            pltpu.VMEM((KVHEADS, length, LANES), BF16),
        ],
        compiler_params=pltpu.CompilerParams(vmem_limit_bytes=48 << 20),
        cost_estimate=pl.CostEstimate(flops=30 * 10**9, bytes_accessed=8 << 20, transcendentals=5 * 10**6),
        name="attention_fwd",
    )(proj, cosine, sine, id_col, id_row)


def attention_bwd_kernel(q_ref, k_ref, v_ref, lse_ref, go_ref, cos_ref, sin_ref, idc_ref, idr_ref, grad_ref, k2_ref, v2_ref, dk_ref, dv_ref, dq_ref):
    length = q_ref.shape[0]
    pairs = AHEADS // 2
    keys = k_ref[...].astype(F32)
    values = v_ref[...].astype(F32)
    low_half = iota((length, LANES), 1) < HDIM
    for head in range(KVHEADS):
        k2_ref[head] = twice(keys, head, low_half).astype(BF16)
        v2_ref[head] = twice(values, head, low_half).astype(BF16)
    dk_ref[...] = jnp.zeros_like(dk_ref)
    dv_ref[...] = jnp.zeros_like(dv_ref)
    scale = HDIM ** (-0.5)
    low_q = iota((QBLOCK, LANES), 1) < HDIM
    zero = jnp.zeros((QBLOCK, LANES), BF16)
    for block in range(length // QBLOCK):
        start, stop = block * QBLOCK, (block + 1) * QBLOCK
        first = max(0, start - LONGEST)
        window = stop - first
        key_pos = iota((window, QBLOCK), 0) + first
        query_pos = iota((window, QBLOCK), 1) + start
        allowed = (idc_ref[first:stop, :] == idr_ref[:, start:stop]) & (query_pos >= key_pos)
        bias = jnp.where(allowed, 0.0, -1e30)
        for pair in range(pairs):
            group = pair * 2 // (AHEADS // KVHEADS)
            cols = slice(pair * LANES, (pair + 1) * LANES)
            query = q_ref[start:stop, cols]
            grad_out = go_ref[start:stop, cols]
            k2 = k2_ref[group, first:stop, :]
            v2 = v2_ref[group, first:stop, :]
            outs = []
            dk = dv = None
            for side in range(2):
                part = jnp.where(low_q, query, zero) if side == 0 else jnp.where(low_q, zero, query)
                grad = jnp.where(low_q, grad_out, zero) if side == 0 else jnp.where(low_q, zero, grad_out)
                head = 2 * pair + side
                scores = dot_nt(k2, part) * scale + bias
                probs = jnp.exp(scores - lse_ref[head : head + 1, start:stop])
                grad_probs = dot_nt(v2, grad)
                product = probs * grad_probs
                inner = jnp.sum(product, axis=0, keepdims=True)
                grad_scores = (product - probs * inner).astype(BF16)
                outs.append(dot_tn(grad_scores, k2))
                more_k = dot_nn(grad_scores, part)
                more_v = dot_nn(probs.astype(BF16), grad)
                dk = more_k if dk is None else dk + more_k
                dv = more_v if dv is None else dv + more_v
            dk_ref[group, first:stop, :] += dk
            dv_ref[group, first:stop, :] += dv
            dq_ref[start:stop, cols] = jnp.where(low_q, outs[0], outs[1]) * scale
    cosine = cos_ref[...]
    sine = sin_ref[...]
    for slab in range(pairs):
        cols = slice(slab * LANES, (slab + 1) * LANES)
        grad_ref[:, cols] = turn(dq_ref[:, cols], cosine, sine, -1.0).astype(BF16)

    def joined(ref):
        both = [ref[head] + pltpu.roll(ref[head], HDIM, 1) for head in range(KVHEADS)]
        return jnp.where(low_half, both[0], both[1])

    at = pairs * LANES
    grad_ref[:, at : at + LANES] = turn(joined(dk_ref) * scale, cosine, sine, -1.0).astype(BF16)
    grad_ref[:, at + LANES : at + 2 * LANES] = joined(dv_ref).astype(BF16)


def attention_bwd(query, keys, values, lse, grad_out, cosine, sine, id_col, id_row):
    length = query.shape[0]
    return pl.pallas_call(
        attention_bwd_kernel,
        out_shape=jax.ShapeDtypeStruct((length, (AHEADS + 2 * KVHEADS) * HDIM), BF16),
        scratch_shapes=[
            pltpu.VMEM((KVHEADS, length, LANES), BF16),
            pltpu.VMEM((KVHEADS, length, LANES), BF16),
            pltpu.VMEM((KVHEADS, length, LANES), F32),
            pltpu.VMEM((KVHEADS, length, LANES), F32),
            pltpu.VMEM((length, AHEADS * HDIM), F32),
        ],
        compiler_params=pltpu.CompilerParams(vmem_limit_bytes=48 << 20),
        cost_estimate=pl.CostEstimate(flops=50 * 10**9, bytes_accessed=8 << 20, transcendentals=5 * 10**6),
        name="attention_bwd",
    )(query, keys, values, lse, grad_out, cosine, sine, id_col, id_row)


def token_marks(ids):
    length = ids.shape[0]
    shape = jnp.arange(length, dtype=jnp.int32)
    columns = []
    for offset in range(1, CONV):
        earlier = jnp.pad(ids, (offset, 0), constant_values=-1)[:length]
        columns.append(earlier == ids)
    for offset in range(1, CONV):
        later = jnp.pad(ids, (0, offset), constant_values=-1)[offset:]
        columns.append(later == ids)
    by_chunk = ids.reshape(-1, CHUNK)
    before = jnp.concatenate([jnp.full((1,), -1, jnp.int32), by_chunk[:-1, -1]])
    columns.append((by_chunk == before[:, None]).reshape(-1))
    columns.append((by_chunk == by_chunk[:, -1:]).reshape(-1))
    columns = [column.astype(F32) for column in columns] + [ids.astype(F32)]
    return jnp.pad(jnp.stack(columns, axis=1), ((0, 0), (0, LANES - len(columns))))


def head_state(step_ref, dtb_ref, rate_ref, marks):
    shape = (CHUNK, CHUNK)
    lower = (iota(shape, 0) >= iota(shape, 1)).astype(F32)
    shifted = step_ref[...] + dtb_ref[0:1, :]
    sizes = softplus(shifted)
    rate = -jnp.exp(rate_ref[0:1, :])
    log_decay = sizes * rate
    totals = dot_nn(lower, log_decay, HIGH)
    entering = jnp.exp(totals) * marks[:, 6:7]
    leaving = jnp.exp(totals[CHUNK - 1 : CHUNK, :] - totals) * marks[:, 7:8]
    return shifted, sizes, rate, log_decay, totals, entering, leaving


def spread(columns, expand):
    stacked = jnp.concatenate(columns, axis=0)
    high, low = split_low(stacked)
    return dot_nn(jnp.concatenate([high, low], axis=1), expand)


def shifted_rows(full, offset, ahead):
    rows = full.shape[0]
    if ahead:
        return pltpu.roll(full, rows - offset, 0)[0:CHUNK]
    return pltpu.roll(full, offset, 0)[8 : 8 + CHUNK]


def halves(values, low_lane):
    return jnp.concatenate(
        [jnp.where(low_lane, values, 0.0), jnp.where(low_lane, 0.0, values)], axis=0
    ).astype(BF16)


def mixer_fwd_kernel(inner, pg_ref, pc_ref, step_ref, marks_ref, row_ref, kern_ref, bias_ref, rate_ref, dtb_ref, skip_ref, gain_ref, expand_ref,
                     scan_ref, start_ref, norm_ref, tail_ref, conv_ref, state_ref, wide_ref, gated_ref):
    channels = pc_ref.shape[1]
    slabs = inner // LANES

    @pl.when(pl.program_id(0) == 0)
    def _():
        tail_ref[...] = jnp.zeros_like(tail_ref)
        state_ref[...] = jnp.zeros_like(state_ref)

    marks = marks_ref[...]
    same = [jnp.broadcast_to(marks[:, j : j + 1], (CHUNK, LANES)) for j in range(CONV - 1)]
    for slab in range(channels // LANES):
        cols = slice(slab * LANES, (slab + 1) * LANES)
        here = pc_ref[:, cols].astype(F32)
        full = jnp.concatenate([tail_ref[:, cols], here], axis=0)
        tail_ref[:, cols] = here[CHUNK - 8 :]
        total = bias_ref[0:1, cols] + kern_ref[CONV - 1 : CONV, cols] * here
        for j in range(1, CONV):
            total = total + kern_ref[CONV - 1 - j : CONV - j, cols] * (same[j - 1] * shifted_rows(full, j, False))
        conv_ref[:, cols] = total * sigmoid(total)

    _, sizes, _, _, totals, entering, leaving = head_state(step_ref, dtb_ref, rate_ref, marks)
    wide_ref[...] = spread([sizes, leaving, entering], expand_ref[...])
    b_low = conv_ref[:, inner : inner + LANES].astype(BF16)
    c_low = conv_ref[:, inner + LANES : inner + 2 * LANES].astype(BF16)
    b_turned = conv_ref[:, inner : inner + LANES].T.astype(BF16)
    shape = (CHUNK, CHUNK)
    together = (marks[:, 8:9] == row_ref[0]) & (iota(shape, 0) >= iota(shape, 1))
    mixing = jnp.where(together, dot_nt(c_low, b_low), 0.0)
    totals_row = totals.T
    low_lane = iota((CHUNK, LANES), 1) < HDIM
    squares = jnp.zeros((CHUNK, LANES), F32)
    for slab in range(slabs):
        cols = slice(slab * LANES, (slab + 1) * LANES)
        parts = []
        for head in (2 * slab, 2 * slab + 1):
            gap = totals[:, head : head + 1] - totals_row[head : head + 1, :]
            parts.append(jnp.exp(jnp.minimum(gap, 0.0)) * mixing)
        both = jnp.concatenate(parts, axis=1).astype(BF16)
        values = conv_ref[:, cols]
        stepped = values * wide_ref[0:CHUNK, cols]
        state = state_ref[:, cols]
        state_low = state.astype(BF16)
        start_ref[0, :, cols] = state_low
        carry = wide_ref[2 * CHUNK : 3 * CHUNK, cols]
        scanned = (
            dot_nn(both, halves(stepped, low_lane))
            + dot_nn(c_low, state_low) * carry
            + skip_ref[0:1, cols] * values
        )
        scan_ref[:, cols] = scanned
        fresh = dot_nn(b_turned, (stepped * wide_ref[CHUNK : 2 * CHUNK, cols]).astype(BF16))
        state_ref[:, cols] = state * carry[CHUNK - 1 :, :] + fresh
        gate = pg_ref[:, cols].astype(F32)
        gated = scanned * (gate * sigmoid(gate))
        gated_ref[:, cols] = gated
        squares = squares + gated * gated
    scale = lax.rsqrt(jnp.sum(squares, axis=1, keepdims=True) / inner + EPS)
    for slab in range(slabs):
        cols = slice(slab * LANES, (slab + 1) * LANES)
        norm_ref[:, cols] = (gated_ref[:, cols] * scale * gain_ref[0:1, cols]).astype(BF16)


def mixer_fwd(gate_part, conv_input, step_raw, marks, rows, kern, bias, rate, dtb, skip, gain, expand):
    length, inner = gate_part.shape
    channels = conv_input.shape[1]
    chunks = length // CHUNK
    shape = jax.ShapeDtypeStruct

    def tokens(width):
        return pl.BlockSpec((CHUNK, width), lambda i: (i, 0))

    def whole(array):
        return pl.BlockSpec(array.shape, lambda i: (0,) * array.ndim)

    return pl.pallas_call(
        partial(mixer_fwd_kernel, inner),
        grid=(chunks,),
        in_specs=[tokens(inner), tokens(channels), tokens(LANES), tokens(LANES), pl.BlockSpec((1, 1, CHUNK), lambda i: (i, 0, 0))]
        + [whole(item) for item in (kern, bias, rate, dtb, skip, gain, expand)],
        out_specs=(tokens(inner), pl.BlockSpec((1, LANES, inner), lambda i: (i, 0, 0)), tokens(inner)),
        out_shape=(shape((length, inner), F32), shape((chunks, LANES, inner), BF16), shape((length, inner), BF16)),
        scratch_shapes=[
            pltpu.VMEM((8, channels), F32),
            pltpu.VMEM((CHUNK, channels), F32),
            pltpu.VMEM((LANES, inner), F32),
            pltpu.VMEM((3 * CHUNK, inner), F32),
            pltpu.VMEM((CHUNK, inner), F32),
        ],
        compiler_params=pltpu.CompilerParams(vmem_limit_bytes=48 << 20),
        cost_estimate=pl.CostEstimate(flops=30 * 10**9, bytes_accessed=20 << 20, transcendentals=8 * 10**6),
        name="mixer_fwd",
    )(gate_part, conv_input, step_raw, marks, rows, kern, bias, rate, dtb, skip, gain, expand)


def mixer_bwd_kernel(inner, chunks, e_ref, pg_ref, pc_ref, before_ref, step_ref, marks_ref, row_ref, scan_ref, start_ref, kern_ref, bias_ref, rate_ref, dtb_ref, skip_ref, gain_ref, expand_ref, gather_ref,
                     dgate_ref, dconv_ref, dstep_ref, dkern_ref, dgain_ref, dskip_ref, dhead_ref,
                     conv_ref, slope_ref, ds_ref, wide_ref, sums_ref, next_ref):
    channels = pc_ref.shape[1]
    slabs = inner // LANES
    step = pl.program_id(0)

    @pl.when(step == 0)
    def _():
        next_ref[...] = jnp.zeros_like(next_ref)
        ds_ref[...] = jnp.zeros_like(ds_ref)
        dkern_ref[...] = jnp.zeros_like(dkern_ref)
        dgain_ref[...] = jnp.zeros_like(dgain_ref)
        dskip_ref[...] = jnp.zeros_like(dskip_ref)
        dhead_ref[...] = jnp.zeros_like(dhead_ref)

    marks = marks_ref[...]
    same = [jnp.broadcast_to(marks[:, j : j + 1], (CHUNK, LANES)) for j in range(CONV - 1)]
    ahead = [jnp.broadcast_to(marks[:, 3 + j : 4 + j], (CHUNK, LANES)) for j in range(CONV - 1)]

    def window(cols):
        here = pc_ref[:, cols].astype(F32)
        return here, jnp.concatenate([before_ref[8:16, cols].astype(F32), here], axis=0)

    for slab in range(channels // LANES):
        cols = slice(slab * LANES, (slab + 1) * LANES)
        here, full = window(cols)
        total = bias_ref[0:1, cols] + kern_ref[CONV - 1 : CONV, cols] * here
        for j in range(1, CONV):
            total = total + kern_ref[CONV - 1 - j : CONV - j, cols] * (same[j - 1] * shifted_rows(full, j, False))
        gate = sigmoid(total)
        conv_ref[:, cols] = total * gate
        slope_ref[:, cols] = gate * (1.0 + total * (1.0 - gate))

    shifted, sizes, rate, log_decay, totals, entering, leaving = head_state(step_ref, dtb_ref, rate_ref, marks)
    wide_ref[...] = spread([sizes, leaving, entering], expand_ref[...])
    b_low = conv_ref[:, inner : inner + LANES].astype(BF16)
    c_low = conv_ref[:, inner + LANES : inner + 2 * LANES].astype(BF16)
    c_turned = conv_ref[:, inner + LANES : inner + 2 * LANES].T.astype(BF16)
    shape = (CHUNK, CHUNK)
    together = (marks[:, 8:9] == row_ref[0]) & (iota(shape, 0) <= iota(shape, 1))
    mixing = jnp.where(together, dot_nt(b_low, c_low), 0.0)
    totals_row = totals.T
    low_lane = iota((CHUNK, LANES), 1) < HDIM

    squares = jnp.zeros((CHUNK, LANES), F32)
    crossed = jnp.zeros((CHUNK, LANES), F32)
    for slab in range(slabs):
        cols = slice(slab * LANES, (slab + 1) * LANES)
        gate = pg_ref[:, cols].astype(F32)
        gated = scan_ref[:, cols] * (gate * sigmoid(gate))
        squares = squares + gated * gated
        crossed = crossed + gated * (gain_ref[0:1, cols] * e_ref[:, cols].astype(F32))
    scale = lax.rsqrt(jnp.sum(squares, axis=1, keepdims=True) / inner + EPS)
    pull = scale * scale * scale * (jnp.sum(crossed, axis=1, keepdims=True) / inner)

    def conv_back(cols, grad):
        pre = grad * slope_ref[:, cols]
        here, full = window(cols)
        behind = jnp.concatenate([pre, next_ref[:, cols]], axis=0)
        next_ref[:, cols] = pre[0:8]
        back = kern_ref[CONV - 1 : CONV, cols] * pre
        dkern_ref[CONV - 1 : CONV, cols] += jnp.sum(pre * here, axis=0, keepdims=True)
        for j in range(1, CONV):
            back = back + kern_ref[CONV - 1 - j : CONV - j, cols] * (ahead[j - 1] * shifted_rows(behind, j, True))
            dkern_ref[CONV - 1 - j : CONV - j, cols] += jnp.sum(
                pre * (same[j - 1] * shifted_rows(full, j, False)), axis=0, keepdims=True
            )
        dkern_ref[CONV : CONV + 1, cols] += jnp.sum(pre, axis=0, keepdims=True)
        dconv_ref[:, cols] = back.astype(BF16)

    d_mixing = jnp.zeros(shape, F32)
    d_b = jnp.zeros(shape, F32)
    d_c = jnp.zeros(shape, F32)
    last_row = iota((CHUNK, LANES), 0) == CHUNK - 1
    for slab in range(slabs):
        cols = slice(slab * LANES, (slab + 1) * LANES)
        gate = pg_ref[:, cols].astype(F32)
        opened = sigmoid(gate)
        silu = gate * opened
        scanned = scan_ref[:, cols]
        error = e_ref[:, cols].astype(F32)
        gated = scanned * silu
        dgain_ref[0:1, cols] += jnp.sum(error * gated * scale, axis=0, keepdims=True)
        d_gated = scale * (gain_ref[0:1, cols] * error) - gated * pull
        dgate_ref[:, cols] = (d_gated * scanned * (opened + silu * (1.0 - opened))).astype(BF16)
        grad = d_gated * silu
        grad_low = grad.astype(BF16)
        values = conv_ref[:, cols]
        size = wide_ref[0:CHUNK, cols]
        leave = wide_ref[CHUNK : 2 * CHUNK, cols]
        enter = wide_ref[2 * CHUNK : 3 * CHUNK, cols]
        stepped = values * size
        stepped_low = stepped.astype(BF16)
        grad_halves = halves(grad, low_lane)
        decays = []
        for head in (2 * slab, 2 * slab + 1):
            gap = totals_row[head : head + 1, :] - totals[:, head : head + 1]
            decays.append(jnp.exp(jnp.minimum(gap, 0.0)))
        both = jnp.concatenate([decay * mixing for decay in decays], axis=1).astype(BF16)
        ds_next = ds_ref[:, cols]
        ds_low = ds_next.astype(BF16)
        left = dot_nn(b_low, ds_low) * leave
        d_stepped = dot_nn(both, grad_halves) + left
        d_both = dot_nt(stepped_low, grad_halves)
        d_mixing = d_mixing + decays[0] * d_both[:, :CHUNK] + decays[1] * d_both[:, CHUNK:]
        entered = (grad * enter).astype(BF16)
        start = start_ref[0, :, cols]
        d_c = d_c + dot_nt(entered, start)
        d_b = d_b + dot_nt((stepped * leave).astype(BF16), ds_low)
        kept = enter[CHUNK - 1 :, :]
        ds_ref[:, cols] = ds_next * kept + dot_nn(c_turned, entered)
        skip = skip_ref[0:1, cols]
        grad_round = grad_low.astype(F32)
        step_round = stepped_low.astype(F32)
        tail = jnp.sum(step_round * left, axis=0, keepdims=True) + kept * jnp.sum(
            ds_next * start.astype(F32), axis=0, keepdims=True
        )
        turns = grad_round * (scanned - skip * values) - step_round * d_stepped
        turns = turns + jnp.where(last_row, tail, 0.0)
        sized = values * d_stepped
        for at, piece in ((0, turns), (1, sized)):
            high, low = split_low(piece)
            sums_ref[at * CHUNK : (at + 1) * CHUNK, cols] = high
            sums_ref[(at + 2) * CHUNK : (at + 3) * CHUNK, cols] = low
        dskip_ref[0:1, cols] += jnp.sum(grad * values, axis=0, keepdims=True)
        conv_back(cols, size * d_stepped + skip * grad)

    heads = dot_nn(sums_ref[...], gather_ref[...])
    heads = heads[0 : 2 * CHUNK] + heads[2 * CHUNK :]
    upper = (iota(shape, 0) <= iota(shape, 1)).astype(F32)
    d_decay = dot_nn(upper, heads[0:CHUNK], HIGH)
    d_sizes = heads[CHUNK:] + d_decay * rate
    d_step = d_sizes * sigmoid(shifted)
    dstep_ref[...] = d_step.astype(BF16)
    dhead_ref[0:1, :] += jnp.sum(d_decay * log_decay, axis=0, keepdims=True)
    dhead_ref[1:2, :] += jnp.sum(d_step, axis=0, keepdims=True)
    d_mixing = jnp.where(together, d_mixing, 0.0)
    d_b = d_b + dot_nn(d_mixing.astype(BF16), c_low)
    d_c = d_c + dot_nn(d_mixing.T.astype(BF16), b_low)
    conv_back(slice(inner, inner + LANES), d_b)
    conv_back(slice(inner + LANES, inner + 2 * LANES), d_c)


def mixer_bwd(error, gate_part, conv_input, step_raw, marks, rows, scanned, starts, kern, bias, rate, dtb, skip, gain, expand, gather):
    length, inner = gate_part.shape
    channels = conv_input.shape[1]
    chunks = length // CHUNK
    shape = jax.ShapeDtypeStruct

    def tokens(width):
        return pl.BlockSpec((CHUNK, width), lambda i: (chunks - 1 - i, 0))

    def whole(array):
        return pl.BlockSpec(array.shape, lambda i: (0,) * len(array.shape))

    per = CHUNK // 16
    sums = (
        shape((8, channels), F32),
        shape((8, inner), F32),
        shape((8, inner), F32),
        shape((8, LANES), F32),
    )
    return pl.pallas_call(
        partial(mixer_bwd_kernel, inner, chunks),
        grid=(chunks,),
        in_specs=[
            tokens(inner),
            tokens(inner),
            tokens(channels),
            pl.BlockSpec((16, channels), lambda i: (jnp.maximum((chunks - 1 - i) * per - 1, 0), 0)),
            tokens(LANES),
            tokens(LANES),
            pl.BlockSpec((1, 1, CHUNK), lambda i: (chunks - 1 - i, 0, 0)),
            tokens(inner),
            pl.BlockSpec((1, LANES, inner), lambda i: (chunks - 1 - i, 0, 0)),
        ]
        + [whole(item) for item in (kern, bias, rate, dtb, skip, gain, expand, gather)],
        out_specs=(tokens(inner), tokens(channels), tokens(LANES)) + tuple(whole(item) for item in sums),
        out_shape=(
            shape((length, inner), BF16),
            shape((length, channels), BF16),
            shape((length, LANES), BF16),
        )
        + sums,
        scratch_shapes=[
            pltpu.VMEM((CHUNK, channels), F32),
            pltpu.VMEM((CHUNK, channels), F32),
            pltpu.VMEM((LANES, inner), F32),
            pltpu.VMEM((3 * CHUNK, inner), F32),
            pltpu.VMEM((4 * CHUNK, inner), BF16),
            pltpu.VMEM((8, channels), F32),
        ],
        compiler_params=pltpu.CompilerParams(vmem_limit_bytes=48 << 20),
        cost_estimate=pl.CostEstimate(flops=70 * 10**9, bytes_accessed=30 << 20, transcendentals=10**7),
        name="mixer_bwd",
    )(error, gate_part, conv_input, conv_input, step_raw, marks, rows, scanned, starts, kern, bias, rate, dtb, skip, gain, expand, gather)


def norm_scale(values):
    return lax.rsqrt(jnp.mean(values * values, axis=-1, keepdims=True) + EPS)


def norm_back(values, scale, gain, error):
    pulled = gain * error
    pull = jnp.mean(values * pulled, axis=-1, keepdims=True)
    grad = scale * pulled - values * (scale * scale * scale * pull)
    return grad, jnp.sum(error * (values * scale), axis=0)


def rotary_tables(length, width):
    half = width // 2
    freq = jnp.exp(-(jnp.arange(half, dtype=F32) * (2.0 / width)) * math.log(THETA))
    angle = jnp.arange(length, dtype=F32)[:, None] * freq[None, :]
    repeats = (1, LANES // half)
    return jnp.tile(jnp.cos(angle), repeats), jnp.tile(jnp.sin(angle), repeats)


def gathered(weight):
    parts = lax.axis_size("rep")
    rows = weight.shape[0] // parts
    mine = lax.dynamic_slice_in_dim(weight, lax.axis_index("rep") * rows, rows, 0)
    return lax.all_gather(mine, ("shard", "rep"), axis=0, tiled=True)


def summed(grad):
    mine = lax.psum_scatter(grad.astype(BF16), ("shard", "rep"), scatter_dimension=0, tiled=True)
    return lax.all_gather(mine, "rep", axis=0, tiled=True).astype(F32)


def shards(
    x_in,
    segment_ids,
    norm_in,
    mix_in,
    attn_in,
    attn_out,
    mix_out,
    norm_ff,
    ff_in,
    ff_out,
    conv_kernel,
    conv_bias,
    log_rate,
    dt_bias,
    skip,
    gate_norm,
    cotangent,
):
    _, length, model = x_in.shape
    inner = gate_norm.shape[0]
    channels = conv_bias.shape[0]
    heads = log_rate.shape[0]
    qkv = attn_in.shape[1]
    lane_pad = LANES - heads

    step_in = jnp.pad(mix_in[:, inner + channels :], ((0, 0), (0, lane_pad)))
    small_in = gathered(jnp.concatenate([attn_in, step_in], axis=1))
    full_norms = lax.all_gather(jnp.stack([norm_in, norm_ff]), "shard", axis=1, tiled=True).astype(F32)
    conv_in = gathered(mix_in[:, inner : inner + channels])
    gate_in = gathered(mix_in[:, :inner])
    full_attn_out = gathered(attn_out)
    full_mix_out = gathered(mix_out)
    full_ff_in = gathered(ff_in)
    full_ff_out = gathered(ff_out)

    ids = segment_ids.reshape(length)
    marks = token_marks(ids)
    id_col = ids.reshape(length, 1)
    id_row = ids.reshape(1, length)
    chunk_rows = ids.astype(F32).reshape(length // CHUNK, 1, CHUNK)
    cosine, sine = rotary_tables(length, HDIM)

    def row(values, pad=0):
        return jnp.pad(values.astype(F32).reshape(1, -1), ((0, 7), (0, pad)))

    kern = jnp.pad(conv_kernel.astype(F32), ((0, 4), (0, 0)))
    bias = row(conv_bias)
    rate = row(log_rate, lane_pad)
    dtb = row(dt_bias, lane_pad)
    skips = row(jnp.repeat(skip, inner // heads))
    gain = row(gate_norm)
    owner = jnp.arange(inner, dtype=jnp.int32) // (inner // heads)
    expand = (owner[None, :] == jnp.arange(LANES, dtype=jnp.int32)[:, None]).astype(BF16)
    gather = expand.T
    expand = jnp.concatenate([expand, expand], axis=0)

    resid = x_in.reshape(length, model).astype(F32)
    first_scale = norm_scale(resid)
    first_low = (resid * first_scale * full_norms[0]).astype(BF16)
    small = dot_nn(first_low, small_in)
    query, keys, values, attended, lse = attention_fwd(small[:, :qkv], cosine, sine, id_col, id_row)
    step_raw = small[:, qkv:]
    conv_input = dot_nn(first_low, conv_in).astype(BF16)
    gate_part = dot_nn(first_low, gate_in).astype(BF16)
    scanned, starts, mixed = mixer_fwd(
        gate_part, conv_input, step_raw, marks, chunk_rows, kern, bias, rate, dtb, skips, gain, expand
    )
    hidden = resid + dot_nt(attended, full_attn_out) + dot_nt(mixed, full_mix_out)
    second_scale = norm_scale(hidden)
    second_low = (hidden * second_scale * full_norms[1]).astype(BF16)
    ff_proj = dot_nn(second_low, full_ff_in)
    width = ff_proj.shape[1] // 2
    opened = sigmoid(ff_proj[:, :width])
    silu = ff_proj[:, :width] * opened
    up = ff_proj[:, width:]
    act_low = (silu * up).astype(BF16)
    output = (hidden + dot_nt(act_low, full_ff_out)).astype(BF16).reshape(x_in.shape)

    grad_out = cotangent.reshape(length, model)
    ff_out_grad = summed(dot_tn(grad_out, act_low))
    grad_act = dot_nn(grad_out, full_ff_out)
    grad_ff = jnp.concatenate(
        [grad_act * up * (opened + silu * (1.0 - opened)), grad_act * silu], axis=1
    ).astype(BF16)
    ff_in_grad = summed(dot_tn(second_low, grad_ff))
    grad_second = dot_nt(grad_ff, full_ff_in)
    grad_hidden, norm_ff_grad = norm_back(hidden, second_scale, full_norms[1], grad_second)
    grad_hidden = grad_hidden + grad_out.astype(F32)
    branch_low = grad_hidden.astype(BF16)
    attn_out_grad = summed(dot_tn(branch_low, attended))
    mix_out_grad = summed(dot_tn(branch_low, mixed))
    grad_attended = dot_nn(branch_low, full_attn_out).astype(BF16)
    grad_mixed = dot_nn(branch_low, full_mix_out).astype(BF16)
    d_gate, d_conv, d_step, d_kern, d_gain, d_skip, d_head = mixer_bwd(
        grad_mixed, gate_part, conv_input, step_raw, marks, chunk_rows, scanned, starts,
        kern, bias, rate, dtb, skips, gain, expand, gather,
    )
    gate_in_grad = dot_tn(first_low, d_gate)
    conv_in_grad = dot_tn(first_low, d_conv)
    grad_attn_proj = attention_bwd(query, keys, values, lse, grad_attended, cosine, sine, id_col, id_row)
    d_small = jnp.concatenate([grad_attn_proj, d_step], axis=1)
    small_in_grad = dot_tn(first_low, d_small)
    gate_sum = summed(gate_in_grad)
    conv_sum = summed(conv_in_grad)
    small_sum = summed(small_in_grad)
    grad_first = dot_nt(d_gate, gate_in) + dot_nt(d_conv, conv_in) + dot_nt(d_small, small_in)
    grad_resid, norm_in_grad = norm_back(resid, first_scale, full_norms[0], grad_first)
    input_grad = (grad_resid + grad_hidden).astype(BF16).reshape(x_in.shape)
    mix_in_grad = jnp.concatenate([gate_sum, conv_sum, small_sum[:, qkv : qkv + heads]], axis=1)
    attn_in_grad = small_sum[:, :qkv]

    pieces = (
        d_kern[:CONV].reshape(-1),
        d_kern[CONV],
        d_gain[0],
        jnp.sum(d_skip[0].reshape(heads, -1), axis=1),
        d_head[0, :heads],
        d_head[1, :heads],
        norm_in_grad,
        norm_ff_grad,
    )
    packed = lax.psum(jnp.concatenate(pieces), ("rep", "shard"))
    split = []
    at = 0
    for piece in pieces:
        split.append(packed[at : at + piece.shape[0]])
        at += piece.shape[0]
    rows = norm_in.shape[0]
    mine = lax.axis_index("shard") * rows
    return (
        output,
        input_grad,
        lax.dynamic_slice_in_dim(split[6], mine, rows, 0),
        mix_in_grad,
        attn_in_grad,
        attn_out_grad,
        mix_out_grad,
        lax.dynamic_slice_in_dim(split[7], mine, rows, 0),
        ff_in_grad,
        ff_out_grad,
        split[0].reshape(conv_kernel.shape),
        split[1],
        split[4],
        split[5],
        split[3],
        split[2],
    )


def solution(mesh):
    in_specs = (
        P(("rep", "shard"), None, None),
        P(("rep", "shard"), None),
        P("shard"),
        P("shard", None),
        P("shard", None),
        P("shard", None),
        P("shard", None),
        P("shard"),
        P("shard", None),
        P("shard", None),
        P(),
        P(),
        P(),
        P(),
        P(),
        P(),
        P(("rep", "shard"), None, None),
    )
    out_specs = (
        P(("rep", "shard"), None, None),
        P(("rep", "shard"), None, None),
        P("shard"),
        P("shard", None),
        P("shard", None),
        P("shard", None),
        P("shard", None),
        P("shard"),
        P("shard", None),
        P("shard", None),
        P(),
        P(),
        P(),
        P(),
        P(),
        P(),
    )
    return jax.shard_map(shards, mesh=mesh, in_specs=in_specs, out_specs=out_specs, check_vma=False)
```

```python
from functools import partial
import math

import jax
import jax.numpy as jnp
from jax import lax
from jax.experimental import pallas as pl
from jax.experimental.pallas import tpu as pltpu
from jax.sharding import PartitionSpec as P

AHEADS = 8
KVHEADS = 2
HDIM = 64
CONV = 4
EPS = 1e-05
THETA = 100000000000.0
HIGH = lax.Precision.HIGHEST
F32 = jnp.float32
BF16 = jnp.bfloat16
LANES = 128
CHUNK = 128
QBLOCK = 256
LONGEST = 512


def dot_nn(left, right, precision=None):
    return lax.dot_general(
        left, right, (((1,), (0,)), ((), ())), precision=precision, preferred_element_type=F32
    )


def dot_nt(left, right):
    return lax.dot_general(left, right, (((1,), (1,)), ((), ())), preferred_element_type=F32)


def dot_tn(left, right):
    return lax.dot_general(left, right, (((0,), (0,)), ((), ())), preferred_element_type=F32)


def sigmoid(values):
    return 0.5 * jnp.tanh(0.5 * values) + 0.5


def softplus(values):
    return jnp.maximum(values, 0.0) + jnp.log1p(jnp.exp(-jnp.abs(values)))


def iota(shape, axis):
    return lax.broadcasted_iota(jnp.int32, shape, axis)


def split_low(values):
    high = values.astype(BF16)
    return high, (values - high.astype(F32)).astype(BF16)


def turn(values, cosine, sine, sign):
    lane = iota(values.shape, 1)
    partner = jnp.where(
        (lane % HDIM) < HDIM // 2,
        -pltpu.roll(values, LANES - HDIM // 2, 1),
        pltpu.roll(values, HDIM // 2, 1),
    )
    return values * cosine + sign * partner * sine


def twice(values, head, low_half):
    swapped = pltpu.roll(values, HDIM, 1)
    return jnp.where(low_half == (head == 0), values, swapped)


def attention_fwd_kernel(proj_ref, cos_ref, sin_ref, idc_ref, idr_ref, q_ref, k_ref, v_ref, out_ref, lse_ref, k2_ref, v2_ref):
    length = proj_ref.shape[0]
    pairs = AHEADS // 2
    cosine = cos_ref[...]
    sine = sin_ref[...]
    for slab in range(pairs):
        cols = slice(slab * LANES, (slab + 1) * LANES)
        q_ref[:, cols] = turn(proj_ref[:, cols], cosine, sine, 1.0).astype(BF16)
    at = pairs * LANES
    keys = turn(proj_ref[:, at : at + LANES], cosine, sine, 1.0)
    values = proj_ref[:, at + LANES : at + 2 * LANES]
    k_ref[...] = keys.astype(BF16)
    v_ref[...] = values.astype(BF16)
    low_half = iota((length, LANES), 1) < HDIM
    for head in range(KVHEADS):
        k2_ref[head] = twice(keys, head, low_half).astype(BF16)
        v2_ref[head] = twice(values, head, low_half).astype(BF16)
    scale = HDIM ** (-0.5)
    low_q = iota((QBLOCK, LANES), 1) < HDIM
    zero = jnp.zeros((QBLOCK, LANES), BF16)
    for block in range(length // QBLOCK):
        start, stop = block * QBLOCK, (block + 1) * QBLOCK
        first = max(0, start - LONGEST)
        window = stop - first
        key_pos = iota((window, QBLOCK), 0) + first
        query_pos = iota((window, QBLOCK), 1) + start
        allowed = (idc_ref[first:stop, 8:9] == idr_ref[:, start:stop]) & (query_pos >= key_pos)
        bias = jnp.where(allowed, 0.0, -1e30)
        for pair in range(pairs):
            group = pair * 2 // (AHEADS // KVHEADS)
            cols = slice(pair * LANES, (pair + 1) * LANES)
            query = q_ref[start:stop, cols]
            k2 = k2_ref[group, first:stop, :]
            v2 = v2_ref[group, first:stop, :]
            outs = []
            for side in range(2):
                part = jnp.where(low_q, query, zero) if side == 0 else jnp.where(low_q, zero, query)
                scores = dot_nt(k2, part) * scale + bias
                top = jnp.max(scores, axis=0, keepdims=True)
                expd = jnp.exp(scores - top)
                total = jnp.sum(expd, axis=0, keepdims=True)
                probs = (expd * (1.0 / total)).astype(BF16)
                outs.append(dot_tn(probs, v2))
                lse_ref[2 * pair + side : 2 * pair + side + 1, start:stop] = top + jnp.log(total)
            out_ref[start:stop, cols] = jnp.where(low_q, outs[0], outs[1]).astype(BF16)


def attention_fwd(proj, cosine, sine, id_col, id_row):
    length = proj.shape[0]
    shape = jax.ShapeDtypeStruct
    return pl.pallas_call(
        attention_fwd_kernel,
        out_shape=(
            shape((length, AHEADS * HDIM), BF16),
            shape((length, LANES), BF16),
            shape((length, LANES), BF16),
            shape((length, AHEADS * HDIM), BF16),
            shape((AHEADS, length), F32),
        ),
        scratch_shapes=[
            pltpu.VMEM((KVHEADS, length, LANES), BF16),
            pltpu.VMEM((KVHEADS, length, LANES), BF16),
        ],
        compiler_params=pltpu.CompilerParams(vmem_limit_bytes=48 << 20),
        cost_estimate=pl.CostEstimate(flops=30 * 10**9, bytes_accessed=8 << 20, transcendentals=5 * 10**6),
        name="attention_fwd",
    )(proj, cosine, sine, id_col, id_row)


def attention_bwd_kernel(n_deps, *refs):
    q_ref, k_ref, v_ref, lse_ref, go_ref, cos_ref, sin_ref, idc_ref, idr_ref = refs[n_deps : n_deps + 9]
    grad_ref, k2_ref, v2_ref, dk_ref, dv_ref, dq_ref = refs[n_deps + 9 :]
    length = q_ref.shape[0]
    pairs = AHEADS // 2
    keys = k_ref[...].astype(F32)
    values = v_ref[...].astype(F32)
    low_half = iota((length, LANES), 1) < HDIM
    for head in range(KVHEADS):
        k2_ref[head] = twice(keys, head, low_half).astype(BF16)
        v2_ref[head] = twice(values, head, low_half).astype(BF16)
    dk_ref[...] = jnp.zeros_like(dk_ref)
    dv_ref[...] = jnp.zeros_like(dv_ref)
    scale = HDIM ** (-0.5)
    low_q = iota((QBLOCK, LANES), 1) < HDIM
    zero = jnp.zeros((QBLOCK, LANES), BF16)
    for block in range(length // QBLOCK):
        start, stop = block * QBLOCK, (block + 1) * QBLOCK
        first = max(0, start - LONGEST)
        window = stop - first
        key_pos = iota((window, QBLOCK), 0) + first
        query_pos = iota((window, QBLOCK), 1) + start
        allowed = (idc_ref[first:stop, 8:9] == idr_ref[:, start:stop]) & (query_pos >= key_pos)
        bias = jnp.where(allowed, 0.0, -1e30)
        for pair in range(pairs):
            group = pair * 2 // (AHEADS // KVHEADS)
            cols = slice(pair * LANES, (pair + 1) * LANES)
            query = q_ref[start:stop, cols]
            grad_out = go_ref[start:stop, cols]
            k2 = k2_ref[group, first:stop, :]
            v2 = v2_ref[group, first:stop, :]
            outs = []
            dk = dv = None
            for side in range(2):
                part = jnp.where(low_q, query, zero) if side == 0 else jnp.where(low_q, zero, query)
                grad = jnp.where(low_q, grad_out, zero) if side == 0 else jnp.where(low_q, zero, grad_out)
                head = 2 * pair + side
                scores = dot_nt(k2, part) * scale + bias
                probs = jnp.exp(scores - lse_ref[head : head + 1, start:stop])
                grad_probs = dot_nt(v2, grad)
                product = probs * grad_probs
                inner = jnp.sum(product, axis=0, keepdims=True)
                grad_scores = (product - probs * inner).astype(BF16)
                outs.append(dot_tn(grad_scores, k2))
                more_k = dot_nn(grad_scores, part)
                more_v = dot_nn(probs.astype(BF16), grad)
                dk = more_k if dk is None else dk + more_k
                dv = more_v if dv is None else dv + more_v
            dk_ref[group, first:stop, :] += dk
            dv_ref[group, first:stop, :] += dv
            dq_ref[start:stop, cols] = jnp.where(low_q, outs[0], outs[1]) * scale
    cosine = cos_ref[...]
    sine = sin_ref[...]
    for slab in range(pairs):
        cols = slice(slab * LANES, (slab + 1) * LANES)
        grad_ref[:, cols] = turn(dq_ref[:, cols], cosine, sine, -1.0).astype(BF16)

    def joined(ref):
        both = [ref[head] + pltpu.roll(ref[head], HDIM, 1) for head in range(KVHEADS)]
        return jnp.where(low_half, both[0], both[1])

    at = pairs * LANES
    grad_ref[:, at : at + LANES] = turn(joined(dk_ref) * scale, cosine, sine, -1.0).astype(BF16)
    grad_ref[:, at + LANES : at + 2 * LANES] = joined(dv_ref).astype(BF16)


def attention_bwd(deps, query, keys, values, lse, grad_out, cosine, sine, id_col, id_row):
    length = query.shape[0]
    return pl.pallas_call(
        partial(attention_bwd_kernel, len(deps)),
        in_specs=[pl.BlockSpec(memory_space=pl.ANY) for _ in deps] + [pl.BlockSpec(memory_space=pltpu.VMEM)] * 9,
        out_shape=jax.ShapeDtypeStruct((length, (AHEADS + 2 * KVHEADS) * HDIM), BF16),
        scratch_shapes=[
            pltpu.VMEM((KVHEADS, length, LANES), BF16),
            pltpu.VMEM((KVHEADS, length, LANES), BF16),
            pltpu.VMEM((KVHEADS, length, LANES), F32),
            pltpu.VMEM((KVHEADS, length, LANES), F32),
            pltpu.VMEM((length, AHEADS * HDIM), F32),
        ],
        compiler_params=pltpu.CompilerParams(vmem_limit_bytes=48 << 20),
        cost_estimate=pl.CostEstimate(flops=50 * 10**9, bytes_accessed=8 << 20, transcendentals=5 * 10**6),
        name="attention_bwd",
    )(*deps, query, keys, values, lse, grad_out, cosine, sine, id_col, id_row)


def gate_cols(slabs, slab):
    half = slabs // 2
    at = slab if slab < half else slab + half
    return slice(at * LANES, (at + 1) * LANES)


def conv_cols(slabs, slab):
    half = slabs // 2
    at = half + slab if slab < half else slabs + slab
    return slice(at * LANES, (at + 1) * LANES)


def token_marks(ids):
    length = ids.shape[0]
    shape = jnp.arange(length, dtype=jnp.int32)
    columns = []
    for offset in range(1, CONV):
        earlier = jnp.pad(ids, (offset, 0), constant_values=-1)[:length]
        columns.append(earlier == ids)
    for offset in range(1, CONV):
        later = jnp.pad(ids, (0, offset), constant_values=-1)[offset:]
        columns.append(later == ids)
    by_chunk = ids.reshape(-1, CHUNK)
    before = jnp.concatenate([jnp.full((1,), -1, jnp.int32), by_chunk[:-1, -1]])
    columns.append((by_chunk == before[:, None]).reshape(-1))
    columns.append((by_chunk == by_chunk[:, -1:]).reshape(-1))
    columns = [column.astype(F32) for column in columns] + [ids.astype(F32)]
    return jnp.pad(jnp.stack(columns, axis=1), ((0, 0), (0, LANES - len(columns))))


def head_state(step_ref, dtb_ref, rate_ref, marks):
    shape = (CHUNK, CHUNK)
    lower = (iota(shape, 0) >= iota(shape, 1)).astype(F32)
    shifted = step_ref[...] + dtb_ref[0:1, :]
    sizes = softplus(shifted)
    rate = -jnp.exp(rate_ref[0:1, :])
    log_decay = sizes * rate
    totals = dot_nn(lower, log_decay, HIGH)
    entering = jnp.exp(totals) * marks[:, 6:7]
    leaving = jnp.exp(totals[CHUNK - 1 : CHUNK, :] - totals) * marks[:, 7:8]
    return shifted, sizes, rate, log_decay, totals, entering, leaving


def spread(columns, expand):
    stacked = jnp.concatenate(columns, axis=0)
    high, low = split_low(stacked)
    return dot_nn(jnp.concatenate([high, low], axis=1), expand)


def shifted_rows(full, offset, ahead):
    rows = full.shape[0]
    if ahead:
        return pltpu.roll(full, rows - offset, 0)[0:CHUNK]
    return pltpu.roll(full, offset, 0)[8 : 8 + CHUNK]


def halves(values, low_lane):
    return jnp.concatenate(
        [jnp.where(low_lane, values, 0.0), jnp.where(low_lane, 0.0, values)], axis=0
    ).astype(BF16)


def mixer_fwd_kernel(inner, proj_ref, step_ref, marks_ref, row_ref, kern_ref, bias_ref, rate_ref, dtb_ref, skip_ref, gain_ref, expand_ref,
                     scan_ref, start_ref, norm_ref, tail_ref, conv_ref, state_ref, wide_ref, gated_ref):
    channels = proj_ref.shape[1] - inner
    slabs = inner // LANES

    @pl.when(pl.program_id(0) == 0)
    def _():
        tail_ref[...] = jnp.zeros_like(tail_ref)
        state_ref[...] = jnp.zeros_like(state_ref)

    marks = marks_ref[...]
    same = [jnp.broadcast_to(marks[:, j : j + 1], (CHUNK, LANES)) for j in range(CONV - 1)]
    for slab in range(channels // LANES):
        cols = slice(slab * LANES, (slab + 1) * LANES)
        here = proj_ref[:, conv_cols(slabs, slab)].astype(F32)
        full = jnp.concatenate([tail_ref[:, cols], here], axis=0)
        tail_ref[:, cols] = here[CHUNK - 8 :]
        total = bias_ref[0:1, cols] + kern_ref[CONV - 1 : CONV, cols] * here
        for j in range(1, CONV):
            total = total + kern_ref[CONV - 1 - j : CONV - j, cols] * (same[j - 1] * shifted_rows(full, j, False))
        conv_ref[:, cols] = total * sigmoid(total)

    _, sizes, _, _, totals, entering, leaving = head_state(step_ref, dtb_ref, rate_ref, marks)
    wide_ref[...] = spread([sizes, leaving, entering], expand_ref[...])
    b_low = conv_ref[:, inner : inner + LANES].astype(BF16)
    c_low = conv_ref[:, inner + LANES : inner + 2 * LANES].astype(BF16)
    b_turned = conv_ref[:, inner : inner + LANES].T.astype(BF16)
    shape = (CHUNK, CHUNK)
    together = (marks[:, 8:9] == row_ref[0]) & (iota(shape, 0) >= iota(shape, 1))
    mixing = jnp.where(together, dot_nt(c_low, b_low), 0.0)
    totals_row = totals.T
    low_lane = iota((CHUNK, LANES), 1) < HDIM
    squares = jnp.zeros((CHUNK, LANES), F32)
    for slab in range(slabs):
        cols = slice(slab * LANES, (slab + 1) * LANES)
        parts = []
        for head in (2 * slab, 2 * slab + 1):
            gap = totals[:, head : head + 1] - totals_row[head : head + 1, :]
            parts.append(jnp.exp(jnp.minimum(gap, 0.0)) * mixing)
        both = jnp.concatenate(parts, axis=1).astype(BF16)
        values = conv_ref[:, cols]
        stepped = values * wide_ref[0:CHUNK, cols]
        state = state_ref[:, cols]
        state_low = state.astype(BF16)
        start_ref[0, :, cols] = state_low
        carry = wide_ref[2 * CHUNK : 3 * CHUNK, cols]
        scanned = (
            dot_nn(both, halves(stepped, low_lane))
            + dot_nn(c_low, state_low) * carry
            + skip_ref[0:1, cols] * values
        )
        scan_ref[:, cols] = scanned
        fresh = dot_nn(b_turned, (stepped * wide_ref[CHUNK : 2 * CHUNK, cols]).astype(BF16))
        state_ref[:, cols] = state * carry[CHUNK - 1 :, :] + fresh
        gate = proj_ref[:, gate_cols(slabs, slab)].astype(F32)
        gated = scanned * (gate * sigmoid(gate))
        gated_ref[:, cols] = gated
        squares = squares + gated * gated
    scale = lax.rsqrt(jnp.sum(squares, axis=1, keepdims=True) / inner + EPS)
    for slab in range(slabs):
        cols = slice(slab * LANES, (slab + 1) * LANES)
        norm_ref[:, cols] = (gated_ref[:, cols] * scale * gain_ref[0:1, cols]).astype(BF16)


def mixer_fwd(projected, step_raw, marks, rows, kern, bias, rate, dtb, skip, gain, expand):
    length, wide = projected.shape
    inner = gain.shape[1]
    channels = wide - inner
    chunks = length // CHUNK
    shape = jax.ShapeDtypeStruct

    def tokens(width):
        return pl.BlockSpec((CHUNK, width), lambda i: (i, 0))

    def whole(array):
        return pl.BlockSpec(array.shape, lambda i: (0,) * array.ndim)

    return pl.pallas_call(
        partial(mixer_fwd_kernel, inner),
        grid=(chunks,),
        in_specs=[tokens(wide), tokens(LANES), tokens(LANES), pl.BlockSpec((1, 1, CHUNK), lambda i: (i, 0, 0))]
        + [whole(item) for item in (kern, bias, rate, dtb, skip, gain, expand)],
        out_specs=(tokens(inner), pl.BlockSpec((1, LANES, inner), lambda i: (i, 0, 0)), tokens(inner)),
        out_shape=(shape((length, inner), F32), shape((chunks, LANES, inner), BF16), shape((length, inner), BF16)),
        scratch_shapes=[
            pltpu.VMEM((8, channels), F32),
            pltpu.VMEM((CHUNK, channels), F32),
            pltpu.VMEM((LANES, inner), F32),
            pltpu.VMEM((3 * CHUNK, inner), F32),
            pltpu.VMEM((CHUNK, inner), F32),
        ],
        compiler_params=pltpu.CompilerParams(vmem_limit_bytes=48 << 20),
        cost_estimate=pl.CostEstimate(flops=30 * 10**9, bytes_accessed=20 << 20, transcendentals=8 * 10**6),
        name="mixer_fwd",
    )(projected, step_raw, marks, rows, kern, bias, rate, dtb, skip, gain, expand)


def mixer_bwd_kernel(inner, second, n_deps, *refs):
    refs = refs[n_deps:]
    e_ref, proj_ref, before_ref, step_ref, marks_ref, row_ref, scan_ref, start_ref = refs[:8]
    kern_ref, bias_ref, rate_ref, dtb_ref, skip_ref, gain_ref, expand_ref, gather_ref = refs[8:16]
    refs = refs[16:]
    if second:
        part_ref, first_ref, refs = refs[0], refs[1], refs[2:]
        dproj_ref = refs[0].at[:, inner:]
        refs[0][:, :inner] = first_ref[...]
        dkern_ref, dgain_ref, dskip_ref, dhead_ref = refs[1:5]
        refs = refs[5:]
    else:
        dproj_ref, dkern_ref, dgain_ref, dskip_ref, dhead_ref, part_ref = refs[:6]
        refs = refs[6:]
    conv_ref, slope_ref, ds_ref, wide_ref, sums_ref, next_ref = refs
    channels = proj_ref.shape[1] - inner
    slabs = inner // LANES
    half = slabs // 2
    base = half if second else 0

    @pl.when(pl.program_id(0) == 0)
    def _():
        next_ref[...] = jnp.zeros_like(next_ref)
        ds_ref[...] = jnp.zeros_like(ds_ref)
        dkern_ref[...] = jnp.zeros_like(dkern_ref)
        dgain_ref[...] = jnp.zeros_like(dgain_ref)
        dskip_ref[...] = jnp.zeros_like(dskip_ref)
        dhead_ref[...] = jnp.zeros_like(dhead_ref)

    marks = marks_ref[...]
    same = [jnp.broadcast_to(marks[:, j : j + 1], (CHUNK, LANES)) for j in range(CONV - 1)]
    ahead = [jnp.broadcast_to(marks[:, 3 + j : 4 + j], (CHUNK, LANES)) for j in range(CONV - 1)]

    def lanes(slab):
        return slice(slab * LANES, (slab + 1) * LANES)

    def window(slab):
        cols = conv_cols(slabs, slab)
        here = proj_ref[:, cols].astype(F32)
        return here, jnp.concatenate([before_ref[8:16, cols].astype(F32), here], axis=0)

    def own(slab):
        return lanes(slab - base if slab < slabs else slab - slabs + half)

    for slab in [base + j for j in range(half)] + [slabs, slabs + 1]:
        cols = lanes(slab)
        here, full = window(slab)
        total = bias_ref[0:1, cols] + kern_ref[CONV - 1 : CONV, cols] * here
        for j in range(1, CONV):
            total = total + kern_ref[CONV - 1 - j : CONV - j, cols] * (same[j - 1] * shifted_rows(full, j, False))
        gate = sigmoid(total)
        conv_ref[:, own(slab)] = total * gate
        if second or slab < slabs:
            slope_ref[:, own(slab)] = gate * (1.0 + total * (1.0 - gate))

    shifted, sizes, rate, log_decay, totals, entering, leaving = head_state(step_ref, dtb_ref, rate_ref, marks)
    wide_ref[...] = spread([sizes, leaving, entering], expand_ref[:, base * LANES : (base + half) * LANES])
    b_values = conv_ref[:, own(slabs)]
    c_values = conv_ref[:, own(slabs + 1)]
    b_low = b_values.astype(BF16)
    c_low = c_values.astype(BF16)
    c_turned = c_values.T.astype(BF16)
    shape = (CHUNK, CHUNK)
    together = (marks[:, 8:9] == row_ref[0]) & (iota(shape, 0) <= iota(shape, 1))
    mixing = jnp.where(together, dot_nt(b_low, c_low), 0.0)
    totals_row = totals.T
    low_lane = iota((CHUNK, LANES), 1) < HDIM

    if second:
        scale = part_ref[:, 3 * LANES : 3 * LANES + 1]
        pull = part_ref[:, 3 * LANES + 1 : 3 * LANES + 2]
        d_mixing = part_ref[:, 0:LANES]
        d_b = part_ref[:, LANES : 2 * LANES]
        d_c = part_ref[:, 2 * LANES : 3 * LANES]
    else:
        squares = jnp.zeros((CHUNK, LANES), F32)
        crossed = jnp.zeros((CHUNK, LANES), F32)
        for slab in range(slabs):
            cols = lanes(slab)
            gate = proj_ref[:, gate_cols(slabs, slab)].astype(F32)
            gated = scan_ref[:, cols] * (gate * sigmoid(gate))
            squares = squares + gated * gated
            crossed = crossed + gated * (gain_ref[0:1, cols] * e_ref[:, cols].astype(F32))
        scale = lax.rsqrt(jnp.sum(squares, axis=1, keepdims=True) / inner + EPS)
        pull = scale * scale * scale * (jnp.sum(crossed, axis=1, keepdims=True) / inner)
        d_mixing = jnp.zeros(shape, F32)
        d_b = jnp.zeros(shape, F32)
        d_c = jnp.zeros(shape, F32)

    def conv_back(slab, grad):
        cols = lanes(slab)
        mine = own(slab)
        pre = grad * slope_ref[:, mine]
        here, full = window(slab)
        behind = jnp.concatenate([pre, next_ref[:, mine]], axis=0)
        next_ref[:, mine] = pre[0:8]
        back = kern_ref[CONV - 1 : CONV, cols] * pre
        dkern_ref[CONV - 1 : CONV, mine] += jnp.sum(pre * here, axis=0, keepdims=True)
        for j in range(1, CONV):
            back = back + kern_ref[CONV - 1 - j : CONV - j, cols] * (ahead[j - 1] * shifted_rows(behind, j, True))
            dkern_ref[CONV - 1 - j : CONV - j, mine] += jnp.sum(
                pre * (same[j - 1] * shifted_rows(full, j, False)), axis=0, keepdims=True
            )
        dkern_ref[CONV : CONV + 1, mine] += jnp.sum(pre, axis=0, keepdims=True)
        dproj_ref[:, half * LANES + mine.start : half * LANES + mine.stop] = back.astype(BF16)

    last_row = iota((CHUNK, LANES), 0) == CHUNK - 1
    for slab in range(base, base + half):
        cols = lanes(slab)
        mine = own(slab)
        gate = proj_ref[:, gate_cols(slabs, slab)].astype(F32)
        opened = sigmoid(gate)
        silu = gate * opened
        scanned = scan_ref[:, cols]
        error = e_ref[:, cols].astype(F32)
        gated = scanned * silu
        dgain_ref[0:1, mine] += jnp.sum(error * gated * scale, axis=0, keepdims=True)
        d_gated = scale * (gain_ref[0:1, cols] * error) - gated * pull
        dproj_ref[:, mine] = (d_gated * scanned * (opened + silu * (1.0 - opened))).astype(BF16)
        grad = d_gated * silu
        grad_low = grad.astype(BF16)
        values = conv_ref[:, mine]
        size = wide_ref[0:CHUNK, mine]
        leave = wide_ref[CHUNK : 2 * CHUNK, mine]
        enter = wide_ref[2 * CHUNK : 3 * CHUNK, mine]
        stepped = values * size
        stepped_low = stepped.astype(BF16)
        grad_halves = halves(grad, low_lane)
        decays = []
        for head in (2 * slab, 2 * slab + 1):
            gap = totals_row[head : head + 1, :] - totals[:, head : head + 1]
            decays.append(jnp.exp(jnp.minimum(gap, 0.0)))
        both = jnp.concatenate([decay * mixing for decay in decays], axis=1).astype(BF16)
        ds_next = ds_ref[:, mine]
        ds_low = ds_next.astype(BF16)
        left = dot_nn(b_low, ds_low) * leave
        d_stepped = dot_nn(both, grad_halves) + left
        d_both = dot_nt(stepped_low, grad_halves)
        d_mixing = d_mixing + decays[0] * d_both[:, :CHUNK] + decays[1] * d_both[:, CHUNK:]
        entered = (grad * enter).astype(BF16)
        start = start_ref[0, :, cols]
        d_c = d_c + dot_nt(entered, start)
        d_b = d_b + dot_nt((stepped * leave).astype(BF16), ds_low)
        kept = enter[CHUNK - 1 :, :]
        ds_ref[:, mine] = ds_next * kept + dot_nn(c_turned, entered)
        skip = skip_ref[0:1, cols]
        grad_round = grad_low.astype(F32)
        step_round = stepped_low.astype(F32)
        tail = jnp.sum(step_round * left, axis=0, keepdims=True) + kept * jnp.sum(
            ds_next * start.astype(F32), axis=0, keepdims=True
        )
        steered = grad_round * (scanned - skip * values) - step_round * d_stepped
        steered = steered + jnp.where(last_row, tail, 0.0)
        sized = values * d_stepped
        for at, piece in ((0, steered), (1, sized)):
            high, low = split_low(piece)
            sums_ref[at * CHUNK : (at + 1) * CHUNK, mine] = high
            sums_ref[(at + 2) * CHUNK : (at + 3) * CHUNK, mine] = low
        dskip_ref[0:1, mine] += jnp.sum(grad * values, axis=0, keepdims=True)
        conv_back(slab, size * d_stepped + skip * grad)

    heads = dot_nn(sums_ref[...], gather_ref[base * LANES : (base + half) * LANES, :])
    heads = heads[0 : 2 * CHUNK] + heads[2 * CHUNK :]
    upper = (iota(shape, 0) <= iota(shape, 1)).astype(F32)
    d_decay = dot_nn(upper, heads[0:CHUNK], HIGH)
    d_sizes = heads[CHUNK:] + d_decay * rate
    d_step = d_sizes * sigmoid(shifted)
    dhead_ref[0:1, :] += jnp.sum(d_decay * log_decay, axis=0, keepdims=True)
    dhead_ref[1:2, :] += jnp.sum(d_step, axis=0, keepdims=True)
    if second:
        d_mixing = jnp.where(together, d_mixing, 0.0)
        d_b = d_b + dot_nn(d_mixing.astype(BF16), c_low)
        d_c = d_c + dot_nn(d_mixing.T.astype(BF16), b_low)
        dproj_ref[:, inner + 2 * LANES :] = (d_step + part_ref[:, 4 * LANES :]).astype(BF16)
        conv_back(slabs, d_b)
        conv_back(slabs + 1, d_c)
    else:
        part_ref[:, 0:LANES] = d_mixing
        part_ref[:, LANES : 2 * LANES] = d_b
        part_ref[:, 2 * LANES : 3 * LANES] = d_c
        part_ref[:, 4 * LANES :] = d_step
        part_ref[:, 3 * LANES : 3 * LANES + 1] = scale
        part_ref[:, 3 * LANES + 1 : 3 * LANES + 2] = pull


def mixer_bwd(second, deps, error, projected, step_raw, marks, rows, scanned, starts, kern, bias, rate, dtb, skip, gain, expand, gather, part=None):
    length, wide = projected.shape
    inner = gain.shape[1]
    chunks = length // CHUNK
    shape = jax.ShapeDtypeStruct

    def tokens(width):
        return pl.BlockSpec((CHUNK, width), lambda i: (chunks - 1 - i, 0))

    def whole(array):
        return pl.BlockSpec(array.shape, lambda i: (0,) * len(array.shape))

    per = CHUNK // 16
    conv = inner // 2 + (2 * LANES if second else 0)
    made = inner + (inner // 2 + conv + LANES if second else 0)
    kept = inner // 2 + 2 * LANES
    sums = (
        shape((8, conv), F32),
        shape((8, inner // 2), F32),
        shape((8, inner // 2), F32),
        shape((8, LANES), F32),
    )
    part_shape = () if second else (shape((length, 5 * LANES), F32),)
    return pl.pallas_call(
        partial(mixer_bwd_kernel, inner, second, len(deps)),
        grid=(chunks,),
        in_specs=[pl.BlockSpec(memory_space=pl.ANY) for _ in deps]
        + [
            tokens(inner),
            tokens(wide),
            pl.BlockSpec((16, wide), lambda i: (jnp.maximum((chunks - 1 - i) * per - 1, 0), 0)),
            tokens(LANES),
            tokens(LANES),
            pl.BlockSpec((1, 1, CHUNK), lambda i: (chunks - 1 - i, 0, 0)),
            tokens(inner),
            pl.BlockSpec((1, LANES, inner), lambda i: (chunks - 1 - i, 0, 0)),
        ]
        + [whole(item) for item in (kern, bias, rate, dtb, skip, gain, expand, gather)]
        + ([tokens(5 * LANES), tokens(inner)] if second else []),
        out_specs=(tokens(made),)
        + tuple(whole(item) for item in sums)
        + (() if second else (tokens(5 * LANES),)),
        out_shape=(shape((length, made), BF16),) + sums + part_shape,
        scratch_shapes=[
            pltpu.VMEM((CHUNK, kept), F32),
            pltpu.VMEM((CHUNK, kept), F32),
            pltpu.VMEM((LANES, inner // 2), F32),
            pltpu.VMEM((3 * CHUNK, inner // 2), F32),
            pltpu.VMEM((4 * CHUNK, inner // 2), BF16),
            pltpu.VMEM((8, kept), F32),
        ],
        compiler_params=pltpu.CompilerParams(vmem_limit_bytes=48 << 20),
        cost_estimate=pl.CostEstimate(flops=30 * 10**9, bytes_accessed=20 << 20, transcendentals=5 * 10**6),
        name="mixer_bwd_second" if second else "mixer_bwd_first",
    )(*deps, error, projected, projected, step_raw, marks, rows, scanned, starts, kern, bias, rate, dtb, skip, gain, expand, gather,
      *(part or ()))


def norm_scale(values):
    return lax.rsqrt(jnp.mean(values * values, axis=-1, keepdims=True) + EPS)


def norm_back(values, scale, gain, error):
    pulled = gain * error
    pull = jnp.mean(values * pulled, axis=-1, keepdims=True)
    grad = scale * pulled - values * (scale * scale * scale * pull)
    return grad, jnp.sum(error * (values * scale), axis=0)


def rotary_tables(length, width):
    half = width // 2
    place = (iota((length, LANES), 1) % half).astype(F32)
    freq = jnp.exp(-(place * (2.0 / width)) * math.log(THETA))
    angle = iota((length, LANES), 0).astype(F32) * freq
    return jnp.cos(angle), jnp.sin(angle)


def places(axis, bit):
    return [(i, i ^ bit) for i in range(lax.axis_size(axis))]


def turns(axis, by):
    size = lax.axis_size(axis)
    return [(i, (i + by) % size) for i in range(size)]


def rep_bits():
    count = lax.axis_size("rep").bit_length() - 1
    return [1 << i for i in range(count)]


def bit_orders(bits):
    rest = bits[1:]
    return rest + bits[:1], rest[::-1] + bits[:1]


def have(bit):
    return (lax.axis_index("rep") & bit) != 0


def my_place(bits):
    place = jnp.int32(0)
    for bit in bits:
        place = place * 2 + have(bit).astype(jnp.int32)
    return place


def nothing(*refs):
    pass


def after(value, *deps):
    if not deps:
        return value
    return pl.pallas_call(
        nothing,
        in_specs=[pl.BlockSpec(memory_space=pl.ANY)] * (1 + len(deps)),
        out_specs=pl.BlockSpec(memory_space=pl.ANY),
        out_shape=jax.ShapeDtypeStruct(value.shape, value.dtype),
        input_output_aliases={0: 0},
        name="after",
    )(value, *deps)


class Moves:
    def start(self, stages):
        self.stages = list(stages)
        self.under_way = None
        self.flying = []

    def advance(self, *deps):
        if self.under_way is not None:
            self.under_way([after(item, *deps) for item in self.flying])
            self.under_way = None
        if self.stages:
            self.flying, self.under_way = self.stages.pop(0)()
        return self

    def finish(self):
        while self.stages or self.under_way is not None:
            self.advance()

    def swap(self, bit, place):
        def send():
            return [
                lax.ppermute(part, "rep", places("rep", own)) for part, own in zip(self.parts, bit)
            ], take

        def take(others):
            parts = []
            for part, other, own in zip(self.parts, others, bit):
                mine = have(own)
                low, high = jnp.where(mine, other, part), jnp.where(mine, part, other)
                parts.append(jnp.concatenate([low, high], axis=place + self.bits.index(own)))
            self.parts = parts

        return send

    def fold(self, bit, place):
        def send():
            return [
                lax.ppermute(side(part, place + self.bits.index(own), own, False), "rep", places("rep", own))
                for part, own in zip(self.parts, bit)
            ], take

        def take(others):
            self.parts = [
                folded(part, other, place + self.bits.index(own), own)
                for part, other, own in zip(self.parts, others, bit)
            ]

        return send


def side(part, axis, bit, mine):
    at = have(bit).astype(jnp.int32)
    return lax.dynamic_slice_in_dim(part, at if mine else 1 - at, 1, axis=axis)


def folded(part, other, axis, bit):
    return (side(part, axis, bit, True).astype(F32) + other.astype(F32)).astype(BF16)


class Gather(Moves):
    def __init__(self, weight):
        self.bits = rep_bits()
        self.groups = lax.axis_size("shard")
        self.shape = (self.groups * weight.shape[0], weight.shape[1])
        self.weight = weight
        self.start([self.over_shard] + [self.swap(bit, 1) for bit in zip(*bit_orders(self.bits))])

    def send_after(self, *deps):
        self.deps = deps
        return self.advance()

    def over_shard(self):
        rows, columns = self.weight.shape[0] >> len(self.bits), self.weight.shape[1]
        mine = lax.dynamic_slice_in_dim(self.weight, my_place(self.bits) * rows, rows, 0)
        mine = after(mine, *self.deps)
        here = lax.axis_index("shard")

        def take(others):
            parts = jnp.zeros((self.groups, rows, columns), self.weight.dtype)
            parts = lax.dynamic_update_slice(parts, mine[None], (here, 0, 0))
            for by, other in enumerate(others, 1):
                parts = lax.dynamic_update_slice(parts, other[None], ((here - by) % self.groups, 0, 0))
            parts = parts.reshape((self.groups,) + (1,) * len(self.bits) + (rows, columns))
            half = self.groups // 2
            self.parts = [parts[:half], parts[half:]] if half else [parts]

        return [lax.ppermute(mine, "shard", turns("shard", by)) for by in range(1, self.groups)], take

    def result(self):
        self.finish()
        return jnp.concatenate(self.parts, axis=0).reshape(self.shape)


class Sum(Moves):
    def __init__(self, *grads):
        self.bits = rep_bits()
        self.groups = lax.axis_size("shard")
        self.rows = grads[0].shape[0] // self.groups >> len(self.bits)
        self.widths = [grad.shape[1] for grad in grads]
        self.columns = sum(self.widths)
        inside = (self.groups,) + (2,) * len(self.bits) + (self.rows,)
        self.grads = [grad.reshape(inside + (grad.shape[1],)) for grad in grads]
        orders = list(zip(*bit_orders(self.bits)))
        self.start(
            [self.over_bit_0]
            + [self.fold(bit, 1) for bit in orders[:-1]]
            + [self.over_shard]
            + [self.swap(bit, 0) for bit in orders]
        )
        self.advance()

    def over_bit_0(self):
        def take(others):
            parts = self.grads
            if self.bits:
                parts = [folded(part, other, 1, self.bits[0]) for part, other in zip(parts, others)]
            part = jnp.concatenate(parts, axis=-1)
            half = self.groups // 2
            self.parts = [part[:half], part[half:]] if half else [part]

        if not self.bits:
            return [], take
        bit = self.bits[0]
        return [lax.ppermute(side(part, 1, bit, False), "rep", places("rep", bit)) for part in self.grads], take

    def over_shard(self):
        part = jnp.concatenate(self.parts, axis=0).reshape(self.groups, self.rows, self.columns)
        here = lax.axis_index("shard")

        def of(by):
            return lax.dynamic_index_in_dim(part, (here + by) % self.groups, 0, keepdims=False)

        def take(others):
            total = of(0).astype(F32)
            for other in others:
                total = total + other.astype(F32)
            mine = total.astype(BF16).reshape((1,) * len(self.bits) + (self.rows, self.columns))
            half = self.rows // 2
            self.parts = [mine[..., :half, :], mine[..., half:, :]]

        return [lax.ppermute(of(by), "shard", turns("shard", by)) for by in range(1, self.groups)], take

    def result(self):
        self.finish()
        whole = jnp.concatenate(self.parts, axis=-2)
        whole = whole.reshape(-1, self.columns).astype(F32)
        ends = [sum(self.widths[: at + 1]) for at in range(len(self.widths))]
        return [whole[:, end - width : end] for end, width in zip(ends, self.widths)]


def gathered(weight):
    parts = lax.axis_size("rep")
    rows = weight.shape[0] // parts
    mine = lax.dynamic_slice_in_dim(weight, lax.axis_index("rep") * rows, rows, 0)
    return lax.all_gather(mine, ("shard", "rep"), axis=0, tiled=True)


def summed_small(values):
    for axis in ("rep", "shard"):
        bit = 1
        while bit < lax.axis_size(axis):
            values = values + lax.ppermute(values, axis, places(axis, bit))
            bit *= 2
    return values


def shards(
    x_in,
    segment_ids,
    norm_in,
    mix_in,
    attn_in,
    attn_out,
    mix_out,
    norm_ff,
    ff_in,
    ff_out,
    conv_kernel,
    conv_bias,
    log_rate,
    dt_bias,
    skip,
    gate_norm,
    cotangent,
):
    _, length, model = x_in.shape
    inner = gate_norm.shape[0]
    channels = conv_bias.shape[0]
    heads = log_rate.shape[0]
    qkv = attn_in.shape[1]
    lane_pad = LANES - heads

    main = inner + channels
    half = inner // 2
    extra = jnp.concatenate([attn_in, jnp.stack([norm_in, norm_ff], axis=1)], axis=1)
    from_small = Gather(jnp.pad(extra, ((0, 0), (0, LANES - 2)))).send_after()
    from_main = Gather(
        jnp.concatenate(
            [
                mix_in[:, :half],
                mix_in[:, inner : inner + half],
                mix_in[:, half:inner],
                mix_in[:, inner + half :],
                jnp.zeros((mix_in.shape[0], lane_pad), BF16),
            ],
            axis=1,
        )
    ).send_after(*from_small.flying)
    small_in = from_small.result()
    main_in = from_main.result()
    outs_wide = attn_out.shape[1] + mix_out.shape[1]
    ff_wide = outs_wide + ff_in.shape[1]
    late = gathered(jnp.concatenate([attn_out, mix_out, ff_in, ff_out], axis=1))
    full_outs = late[:, :outs_wide]
    full_ff_in = late[:, outs_wide:ff_wide]
    full_ff_out = late[:, ff_wide:]

    ids = segment_ids.reshape(length)
    marks = token_marks(ids)
    id_row = ids.astype(F32).reshape(1, length)
    chunk_rows = ids.astype(F32).reshape(length // CHUNK, 1, CHUNK)
    cosine, sine = rotary_tables(length, HDIM)

    def row(values, pad=0):
        return jnp.pad(values.astype(F32).reshape(1, -1), ((0, 7), (0, pad)))

    kern = jnp.pad(conv_kernel.astype(F32), ((0, 4), (0, 0)))
    bias = row(conv_bias)
    rate = row(log_rate, lane_pad)
    dtb = row(dt_bias, lane_pad)
    skips = row(jnp.repeat(skip, inner // heads))
    gain = row(gate_norm)
    owner = jnp.arange(inner, dtype=jnp.int32) // (inner // heads)
    expand = (owner[None, :] == jnp.arange(LANES, dtype=jnp.int32)[:, None]).astype(BF16)
    gather = expand.T
    expand = jnp.concatenate([expand, expand], axis=0)

    resid = x_in.reshape(length, model).astype(F32)
    full_norms = small_in[:, qkv : qkv + 2].astype(F32).T
    first_scale = norm_scale(resid)
    first_low = (resid * first_scale * full_norms[0]).astype(BF16)
    attn_proj = dot_nn(first_low, small_in[:, :qkv])
    query, keys, values, attended, lse = attention_fwd(attn_proj, cosine, sine, marks, id_row)
    step_raw = dot_nn(first_low, main_in[:, main:])
    projected = dot_nn(first_low, main_in[:, :main]).astype(BF16)
    scanned, starts, mixed = mixer_fwd(
        projected, step_raw, marks, chunk_rows, kern, bias, rate, dtb, skips, gain, expand
    )
    attw = attended.shape[1]
    branches = jnp.concatenate([attended, mixed], axis=1)
    hidden = resid + dot_nt(branches, full_outs)
    second_scale = norm_scale(hidden)
    second_low = (hidden * second_scale * full_norms[1]).astype(BF16)
    ff_proj = dot_nn(second_low, full_ff_in)
    width = ff_proj.shape[1] // 2
    opened = sigmoid(ff_proj[:, :width])
    silu = ff_proj[:, :width] * opened
    up = ff_proj[:, width:]
    act_low = (silu * up).astype(BF16)
    output = (hidden + dot_nt(act_low, full_ff_out)).astype(BF16).reshape(x_in.shape)

    grad_out = cotangent.reshape(length, model)
    ff_out_part = dot_tn(grad_out, act_low).astype(BF16)
    grad_act = dot_nn(grad_out, full_ff_out)
    grad_ff = jnp.concatenate(
        [grad_act * up * (opened + silu * (1.0 - opened)), grad_act * silu], axis=1
    ).astype(BF16)
    sum_ff = Sum(ff_out_part, dot_tn(second_low, grad_ff).astype(BF16))
    grad_second = dot_nt(grad_ff, full_ff_in)
    grad_hidden, norm_ff_grad = norm_back(hidden, second_scale, full_norms[1], grad_second)
    grad_hidden = grad_hidden + grad_out.astype(F32)
    branch_low = grad_hidden.astype(BF16)
    sum_ff.advance(branch_low)
    outs_part = dot_tn(branch_low, branches).astype(BF16)
    grad_branches = dot_nn(branch_low, full_outs).astype(BF16)
    d_attn = attention_bwd(
        sum_ff.parts, query, keys, values, lse, grad_branches[:, :attw], cosine, sine, marks, id_row
    )
    sum_ff.advance(d_attn)
    sum_mid = Sum(outs_part, dot_tn(first_low, d_attn).astype(BF16))
    common = (step_raw, marks, chunk_rows, scanned, starts, kern, bias, rate, dtb, skips, gain, expand, gather)
    d_first, d_kern_a, d_gain_a, d_skip_a, d_head_a, handed = mixer_bwd(
        False, sum_ff.parts, grad_branches[:, attw:], projected, *common
    )
    sum_ff.advance(d_first)
    sum_mid.advance(d_first)
    d_main, d_kern_b, d_gain_b, d_skip_b, d_head_b = mixer_bwd(
        True, sum_ff.parts + sum_mid.parts, grad_branches[:, attw:], projected, *common, part=(handed, d_first)
    )
    sum_ff.advance(d_main)
    sum_mid.advance(d_main)
    sum_main = Sum(dot_tn(first_low, d_main).astype(BF16))
    grad_first = dot_nt(d_main, main_in) + dot_nt(d_attn, small_in[:, :qkv])
    grad_resid, norm_in_grad = norm_back(resid, first_scale, full_norms[0], grad_first)
    input_grad = (grad_resid + grad_hidden).astype(BF16).reshape(x_in.shape)
    sums = (sum_ff, sum_mid, sum_main)
    while any(item.stages for item in sums):
        for item in sums:
            item.advance()
    ff_out_grad, ff_in_grad = sum_ff.result()
    outs_sum, attn_in_grad = sum_mid.result()
    main_sum = sum_main.result()[0]
    mix_in_grad = jnp.concatenate(
        [
            main_sum[:, :half],
            main_sum[:, inner : inner + half],
            main_sum[:, half:inner],
            main_sum[:, inner + half : main + heads],
        ],
        axis=1,
    )
    d_kern = jnp.concatenate([d_kern_a, d_kern_b], axis=1)
    d_gain = jnp.concatenate([d_gain_a, d_gain_b], axis=1)
    d_skip = jnp.concatenate([d_skip_a, d_skip_b], axis=1)
    d_head = d_head_a + d_head_b

    pieces = (
        d_kern[:CONV].reshape(-1),
        d_kern[CONV],
        d_gain[0],
        jnp.sum(d_skip[0].reshape(heads, -1), axis=1),
        d_head[0, :heads],
        d_head[1, :heads],
        norm_in_grad,
        norm_ff_grad,
    )
    packed = summed_small(jnp.concatenate(pieces))
    split = []
    at = 0
    for piece in pieces:
        split.append(packed[at : at + piece.shape[0]])
        at += piece.shape[0]
    rows = norm_in.shape[0]
    mine = lax.axis_index("shard") * rows
    return (
        output,
        input_grad,
        lax.dynamic_slice_in_dim(split[6], mine, rows, 0),
        mix_in_grad,
        attn_in_grad,
        outs_sum[:, :attw],
        outs_sum[:, attw:],
        lax.dynamic_slice_in_dim(split[7], mine, rows, 0),
        ff_in_grad,
        ff_out_grad,
        split[0].reshape(conv_kernel.shape),
        split[1],
        split[4],
        split[5],
        split[3],
        split[2],
    )


def solution(mesh):
    in_specs = (
        P(("rep", "shard"), None, None),
        P(("rep", "shard"), None),
        P("shard"),
        P("shard", None),
        P("shard", None),
        P("shard", None),
        P("shard", None),
        P("shard"),
        P("shard", None),
        P("shard", None),
        P(),
        P(),
        P(),
        P(),
        P(),
        P(),
        P(("rep", "shard"), None, None),
    )
    out_specs = (
        P(("rep", "shard"), None, None),
        P(("rep", "shard"), None, None),
        P("shard"),
        P("shard", None),
        P("shard", None),
        P("shard", None),
        P("shard", None),
        P("shard"),
        P("shard", None),
        P("shard", None),
        P(),
        P(),
        P(),
        P(),
        P(),
        P(),
    )
    return jax.shard_map(shards, mesh=mesh, in_specs=in_specs, out_specs=out_specs, check_vma=False)
```

```python
from functools import partial
import math

import jax
import jax.numpy as jnp
from jax import lax
from jax.experimental import pallas as pl
from jax.experimental.pallas import tpu as pltpu
from jax.sharding import PartitionSpec as P

AHEADS = 8
KVHEADS = 2
HDIM = 64
CONV = 4
EPS = 1e-05
THETA = 100000000000.0
HIGH = lax.Precision.HIGHEST
F32 = jnp.float32
BF16 = jnp.bfloat16
LANES = 128
CHUNK = 128
QBLOCK = 256
LONGEST = 512


def dot_nn(left, right, precision=None):
    return lax.dot_general(
        left, right, (((1,), (0,)), ((), ())), precision=precision, preferred_element_type=F32
    )


def dot_nt(left, right):
    return lax.dot_general(left, right, (((1,), (1,)), ((), ())), preferred_element_type=F32)


def dot_tn(left, right):
    return lax.dot_general(left, right, (((0,), (0,)), ((), ())), preferred_element_type=F32)


def sigmoid(values):
    return 0.5 * jnp.tanh(0.5 * values) + 0.5


def softplus(values):
    return jnp.maximum(values, 0.0) + jnp.log1p(jnp.exp(-jnp.abs(values)))


def iota(shape, axis):
    return lax.broadcasted_iota(jnp.int32, shape, axis)


def split_low(values):
    high = values.astype(BF16)
    return high, (values - high.astype(F32)).astype(BF16)


def turn(values, cosine, sine, sign):
    lane = iota(values.shape, 1)
    partner = jnp.where(
        (lane % HDIM) < HDIM // 2,
        -pltpu.roll(values, LANES - HDIM // 2, 1),
        pltpu.roll(values, HDIM // 2, 1),
    )
    return values * cosine + sign * partner * sine


def twice(values, head, low_half):
    swapped = pltpu.roll(values, HDIM, 1)
    return jnp.where(low_half == (head == 0), values, swapped)


def attention_fwd_kernel(proj_ref, cos_ref, sin_ref, idc_ref, idr_ref, q_ref, k_ref, v_ref, out_ref, lse_ref, k2_ref, v2_ref):
    length = proj_ref.shape[0]
    pairs = AHEADS // 2
    cosine = cos_ref[...]
    sine = sin_ref[...]
    for slab in range(pairs):
        cols = slice(slab * LANES, (slab + 1) * LANES)
        q_ref[:, cols] = turn(proj_ref[:, cols], cosine, sine, 1.0).astype(BF16)
    at = pairs * LANES
    keys = turn(proj_ref[:, at : at + LANES], cosine, sine, 1.0)
    values = proj_ref[:, at + LANES : at + 2 * LANES]
    k_ref[...] = keys.astype(BF16)
    v_ref[...] = values.astype(BF16)
    low_half = iota((length, LANES), 1) < HDIM
    for head in range(KVHEADS):
        k2_ref[head] = twice(keys, head, low_half).astype(BF16)
        v2_ref[head] = twice(values, head, low_half).astype(BF16)
    scale = HDIM ** (-0.5)
    low_q = iota((QBLOCK, LANES), 1) < HDIM
    zero = jnp.zeros((QBLOCK, LANES), BF16)
    for block in range(length // QBLOCK):
        start, stop = block * QBLOCK, (block + 1) * QBLOCK
        first = max(0, start - LONGEST)
        window = stop - first
        key_pos = iota((window, QBLOCK), 0) + first
        query_pos = iota((window, QBLOCK), 1) + start
        allowed = (idc_ref[first:stop, 8:9] == idr_ref[:, start:stop]) & (query_pos >= key_pos)
        bias = jnp.where(allowed, 0.0, -1e30)
        for pair in range(pairs):
            group = pair * 2 // (AHEADS // KVHEADS)
            cols = slice(pair * LANES, (pair + 1) * LANES)
            query = q_ref[start:stop, cols]
            k2 = k2_ref[group, first:stop, :]
            v2 = v2_ref[group, first:stop, :]
            outs = []
            for side in range(2):
                part = jnp.where(low_q, query, zero) if side == 0 else jnp.where(low_q, zero, query)
                scores = dot_nt(k2, part) * scale + bias
                top = jnp.max(scores, axis=0, keepdims=True)
                expd = jnp.exp(scores - top)
                total = jnp.sum(expd, axis=0, keepdims=True)
                probs = (expd * (1.0 / total)).astype(BF16)
                outs.append(dot_tn(probs, v2))
                lse_ref[2 * pair + side : 2 * pair + side + 1, start:stop] = top + jnp.log(total)
            out_ref[start:stop, cols] = jnp.where(low_q, outs[0], outs[1]).astype(BF16)


def attention_fwd(proj, cosine, sine, id_col, id_row):
    length = proj.shape[0]
    shape = jax.ShapeDtypeStruct
    return pl.pallas_call(
        attention_fwd_kernel,
        out_shape=(
            shape((length, AHEADS * HDIM), BF16),
            shape((length, LANES), BF16),
            shape((length, LANES), BF16),
            shape((length, AHEADS * HDIM), BF16),
            shape((AHEADS, length), F32),
        ),
        scratch_shapes=[
            pltpu.VMEM((KVHEADS, length, LANES), BF16),
            pltpu.VMEM((KVHEADS, length, LANES), BF16),
        ],
        compiler_params=pltpu.CompilerParams(vmem_limit_bytes=48 << 20),
        cost_estimate=pl.CostEstimate(flops=30 * 10**9, bytes_accessed=8 << 20, transcendentals=5 * 10**6),
        name="attention_fwd",
    )(proj, cosine, sine, id_col, id_row)


def attention_bwd_kernel(n_deps, *refs):
    q_ref, k_ref, v_ref, lse_ref, go_ref, cos_ref, sin_ref, idc_ref, idr_ref = refs[n_deps : n_deps + 9]
    grad_ref, k2_ref, v2_ref, dk_ref, dv_ref, dq_ref = refs[n_deps + 9 :]
    length = q_ref.shape[0]
    pairs = AHEADS // 2
    keys = k_ref[...].astype(F32)
    values = v_ref[...].astype(F32)
    low_half = iota((length, LANES), 1) < HDIM
    for head in range(KVHEADS):
        k2_ref[head] = twice(keys, head, low_half).astype(BF16)
        v2_ref[head] = twice(values, head, low_half).astype(BF16)
    dk_ref[...] = jnp.zeros_like(dk_ref)
    dv_ref[...] = jnp.zeros_like(dv_ref)
    scale = HDIM ** (-0.5)
    low_q = iota((QBLOCK, LANES), 1) < HDIM
    zero = jnp.zeros((QBLOCK, LANES), BF16)
    for block in range(length // QBLOCK):
        start, stop = block * QBLOCK, (block + 1) * QBLOCK
        first = max(0, start - LONGEST)
        window = stop - first
        key_pos = iota((window, QBLOCK), 0) + first
        query_pos = iota((window, QBLOCK), 1) + start
        allowed = (idc_ref[first:stop, 8:9] == idr_ref[:, start:stop]) & (query_pos >= key_pos)
        bias = jnp.where(allowed, 0.0, -1e30)
        for pair in range(pairs):
            group = pair * 2 // (AHEADS // KVHEADS)
            cols = slice(pair * LANES, (pair + 1) * LANES)
            query = q_ref[start:stop, cols]
            grad_out = go_ref[start:stop, cols]
            k2 = k2_ref[group, first:stop, :]
            v2 = v2_ref[group, first:stop, :]
            outs = []
            dk = dv = None
            for side in range(2):
                part = jnp.where(low_q, query, zero) if side == 0 else jnp.where(low_q, zero, query)
                grad = jnp.where(low_q, grad_out, zero) if side == 0 else jnp.where(low_q, zero, grad_out)
                head = 2 * pair + side
                scores = dot_nt(k2, part) * scale + bias
                probs = jnp.exp(scores - lse_ref[head : head + 1, start:stop])
                grad_probs = dot_nt(v2, grad)
                product = probs * grad_probs
                inner = jnp.sum(product, axis=0, keepdims=True)
                grad_scores = (product - probs * inner).astype(BF16)
                outs.append(dot_tn(grad_scores, k2))
                more_k = dot_nn(grad_scores, part)
                more_v = dot_nn(probs.astype(BF16), grad)
                dk = more_k if dk is None else dk + more_k
                dv = more_v if dv is None else dv + more_v
            dk_ref[group, first:stop, :] += dk
            dv_ref[group, first:stop, :] += dv
            dq_ref[start:stop, cols] = jnp.where(low_q, outs[0], outs[1]) * scale
    cosine = cos_ref[...]
    sine = sin_ref[...]
    for slab in range(pairs):
        cols = slice(slab * LANES, (slab + 1) * LANES)
        grad_ref[:, cols] = turn(dq_ref[:, cols], cosine, sine, -1.0).astype(BF16)

    def joined(ref):
        both = [ref[head] + pltpu.roll(ref[head], HDIM, 1) for head in range(KVHEADS)]
        return jnp.where(low_half, both[0], both[1])

    at = pairs * LANES
    grad_ref[:, at : at + LANES] = turn(joined(dk_ref) * scale, cosine, sine, -1.0).astype(BF16)
    grad_ref[:, at + LANES : at + 2 * LANES] = joined(dv_ref).astype(BF16)


def attention_bwd(deps, query, keys, values, lse, grad_out, cosine, sine, id_col, id_row):
    length = query.shape[0]
    return pl.pallas_call(
        partial(attention_bwd_kernel, len(deps)),
        in_specs=[pl.BlockSpec(memory_space=pl.ANY) for _ in deps] + [pl.BlockSpec(memory_space=pltpu.VMEM)] * 9,
        out_shape=jax.ShapeDtypeStruct((length, (AHEADS + 2 * KVHEADS) * HDIM), BF16),
        scratch_shapes=[
            pltpu.VMEM((KVHEADS, length, LANES), BF16),
            pltpu.VMEM((KVHEADS, length, LANES), BF16),
            pltpu.VMEM((KVHEADS, length, LANES), F32),
            pltpu.VMEM((KVHEADS, length, LANES), F32),
            pltpu.VMEM((length, AHEADS * HDIM), F32),
        ],
        compiler_params=pltpu.CompilerParams(vmem_limit_bytes=48 << 20),
        cost_estimate=pl.CostEstimate(flops=50 * 10**9, bytes_accessed=8 << 20, transcendentals=5 * 10**6),
        name="attention_bwd",
    )(*deps, query, keys, values, lse, grad_out, cosine, sine, id_col, id_row)


def gate_cols(slabs, slab):
    half = slabs // 2
    at = slab if slab < half else slab + half
    return slice(at * LANES, (at + 1) * LANES)


def conv_cols(slabs, slab):
    half = slabs // 2
    at = half + slab if slab < half else slabs + slab
    return slice(at * LANES, (at + 1) * LANES)


def token_marks(ids):
    length = ids.shape[0]
    shape = jnp.arange(length, dtype=jnp.int32)
    columns = []
    for offset in range(1, CONV):
        earlier = jnp.pad(ids, (offset, 0), constant_values=-1)[:length]
        columns.append(earlier == ids)
    for offset in range(1, CONV):
        later = jnp.pad(ids, (0, offset), constant_values=-1)[offset:]
        columns.append(later == ids)
    by_chunk = ids.reshape(-1, CHUNK)
    before = jnp.concatenate([jnp.full((1,), -1, jnp.int32), by_chunk[:-1, -1]])
    columns.append((by_chunk == before[:, None]).reshape(-1))
    columns.append((by_chunk == by_chunk[:, -1:]).reshape(-1))
    columns = [column.astype(F32) for column in columns] + [ids.astype(F32)]
    return jnp.pad(jnp.stack(columns, axis=1), ((0, 0), (0, LANES - len(columns))))


def head_state(step_ref, dtb_ref, rate_ref, marks):
    shape = (CHUNK, CHUNK)
    lower = (iota(shape, 0) >= iota(shape, 1)).astype(F32)
    shifted = step_ref[...] + dtb_ref[0:1, :]
    sizes = softplus(shifted)
    rate = -jnp.exp(rate_ref[0:1, :])
    log_decay = sizes * rate
    totals = dot_nn(lower, log_decay, HIGH)
    entering = jnp.exp(totals) * marks[:, 6:7]
    leaving = jnp.exp(totals[CHUNK - 1 : CHUNK, :] - totals) * marks[:, 7:8]
    return shifted, sizes, rate, log_decay, totals, entering, leaving


def spread(columns, expand):
    stacked = jnp.concatenate(columns, axis=0)
    high, low = split_low(stacked)
    return dot_nn(jnp.concatenate([high, low], axis=1), expand)


def shifted_rows(full, offset, ahead):
    rows = full.shape[0]
    if ahead:
        return pltpu.roll(full, rows - offset, 0)[0:CHUNK]
    return pltpu.roll(full, offset, 0)[8 : 8 + CHUNK]


def halves(values, low_lane):
    return jnp.concatenate(
        [jnp.where(low_lane, values, 0.0), jnp.where(low_lane, 0.0, values)], axis=0
    ).astype(BF16)


def mixer_fwd_kernel(inner, proj_ref, step_ref, marks_ref, row_ref, kern_ref, bias_ref, rate_ref, dtb_ref, skip_ref, gain_ref, expand_ref,
                     scan_ref, start_ref, norm_ref, tail_ref, conv_ref, state_ref, wide_ref, gated_ref):
    channels = proj_ref.shape[1] - inner
    slabs = inner // LANES

    @pl.when(pl.program_id(0) == 0)
    def _():
        tail_ref[...] = jnp.zeros_like(tail_ref)
        state_ref[...] = jnp.zeros_like(state_ref)

    marks = marks_ref[...]
    same = [jnp.broadcast_to(marks[:, j : j + 1], (CHUNK, LANES)) for j in range(CONV - 1)]
    for slab in range(channels // LANES):
        cols = slice(slab * LANES, (slab + 1) * LANES)
        here = proj_ref[:, conv_cols(slabs, slab)].astype(F32)
        full = jnp.concatenate([tail_ref[:, cols], here], axis=0)
        tail_ref[:, cols] = here[CHUNK - 8 :]
        total = bias_ref[0:1, cols] + kern_ref[CONV - 1 : CONV, cols] * here
        for j in range(1, CONV):
            total = total + kern_ref[CONV - 1 - j : CONV - j, cols] * (same[j - 1] * shifted_rows(full, j, False))
        conv_ref[:, cols] = total * sigmoid(total)

    _, sizes, _, _, totals, entering, leaving = head_state(step_ref, dtb_ref, rate_ref, marks)
    wide_ref[...] = spread([sizes, leaving, entering], expand_ref[...])
    b_low = conv_ref[:, inner : inner + LANES].astype(BF16)
    c_low = conv_ref[:, inner + LANES : inner + 2 * LANES].astype(BF16)
    b_turned = conv_ref[:, inner : inner + LANES].T.astype(BF16)
    shape = (CHUNK, CHUNK)
    together = (marks[:, 8:9] == row_ref[0]) & (iota(shape, 0) >= iota(shape, 1))
    mixing = jnp.where(together, dot_nt(c_low, b_low), 0.0)
    totals_row = totals.T
    low_lane = iota((CHUNK, LANES), 1) < HDIM
    squares = jnp.zeros((CHUNK, LANES), F32)
    for slab in range(slabs):
        cols = slice(slab * LANES, (slab + 1) * LANES)
        parts = []
        for head in (2 * slab, 2 * slab + 1):
            gap = totals[:, head : head + 1] - totals_row[head : head + 1, :]
            parts.append(jnp.exp(jnp.minimum(gap, 0.0)) * mixing)
        both = jnp.concatenate(parts, axis=1).astype(BF16)
        values = conv_ref[:, cols]
        stepped = values * wide_ref[0:CHUNK, cols]
        state = state_ref[:, cols]
        state_low = state.astype(BF16)
        start_ref[0, :, cols] = state_low
        carry = wide_ref[2 * CHUNK : 3 * CHUNK, cols]
        scanned = (
            dot_nn(both, halves(stepped, low_lane))
            + dot_nn(c_low, state_low) * carry
            + skip_ref[0:1, cols] * values
        )
        scan_ref[:, cols] = scanned
        fresh = dot_nn(b_turned, (stepped * wide_ref[CHUNK : 2 * CHUNK, cols]).astype(BF16))
        state_ref[:, cols] = state * carry[CHUNK - 1 :, :] + fresh
        gate = proj_ref[:, gate_cols(slabs, slab)].astype(F32)
        gated = scanned * (gate * sigmoid(gate))
        gated_ref[:, cols] = gated
        squares = squares + gated * gated
    scale = lax.rsqrt(jnp.sum(squares, axis=1, keepdims=True) / inner + EPS)
    for slab in range(slabs):
        cols = slice(slab * LANES, (slab + 1) * LANES)
        norm_ref[:, cols] = (gated_ref[:, cols] * scale * gain_ref[0:1, cols]).astype(BF16)


def mixer_fwd(projected, step_raw, marks, rows, kern, bias, rate, dtb, skip, gain, expand):
    length, wide = projected.shape
    inner = gain.shape[1]
    channels = wide - inner
    chunks = length // CHUNK
    shape = jax.ShapeDtypeStruct

    def tokens(width):
        return pl.BlockSpec((CHUNK, width), lambda i: (i, 0))

    def whole(array):
        return pl.BlockSpec(array.shape, lambda i: (0,) * array.ndim)

    return pl.pallas_call(
        partial(mixer_fwd_kernel, inner),
        grid=(chunks,),
        in_specs=[tokens(wide), tokens(LANES), tokens(LANES), pl.BlockSpec((1, 1, CHUNK), lambda i: (i, 0, 0))]
        + [whole(item) for item in (kern, bias, rate, dtb, skip, gain, expand)],
        out_specs=(tokens(inner), pl.BlockSpec((1, LANES, inner), lambda i: (i, 0, 0)), tokens(inner)),
        out_shape=(shape((length, inner), F32), shape((chunks, LANES, inner), BF16), shape((length, inner), BF16)),
        scratch_shapes=[
            pltpu.VMEM((8, channels), F32),
            pltpu.VMEM((CHUNK, channels), F32),
            pltpu.VMEM((LANES, inner), F32),
            pltpu.VMEM((3 * CHUNK, inner), F32),
            pltpu.VMEM((CHUNK, inner), F32),
        ],
        compiler_params=pltpu.CompilerParams(vmem_limit_bytes=48 << 20),
        cost_estimate=pl.CostEstimate(flops=30 * 10**9, bytes_accessed=20 << 20, transcendentals=8 * 10**6),
        name="mixer_fwd",
    )(projected, step_raw, marks, rows, kern, bias, rate, dtb, skip, gain, expand)


def mixer_bwd_kernel(inner, second, n_deps, *refs):
    refs = refs[n_deps:]
    e_ref, proj_ref, before_ref, step_ref, marks_ref, row_ref, scan_ref, start_ref = refs[:8]
    kern_ref, bias_ref, rate_ref, dtb_ref, skip_ref, gain_ref, expand_ref, gather_ref = refs[8:16]
    refs = refs[16:]
    if second:
        part_ref, first_ref, refs = refs[0], refs[1], refs[2:]
        dproj_ref = refs[0].at[:, inner:]
        refs[0][:, :inner] = first_ref[...]
        dkern_ref, dgain_ref, dskip_ref, dhead_ref = refs[1:5]
        refs = refs[5:]
    else:
        dproj_ref, dkern_ref, dgain_ref, dskip_ref, dhead_ref, part_ref = refs[:6]
        refs = refs[6:]
    conv_ref, slope_ref, ds_ref, wide_ref, sums_ref, next_ref = refs
    channels = proj_ref.shape[1] - inner
    slabs = inner // LANES
    half = slabs // 2
    base = half if second else 0

    @pl.when(pl.program_id(0) == 0)
    def _():
        next_ref[...] = jnp.zeros_like(next_ref)
        ds_ref[...] = jnp.zeros_like(ds_ref)
        dkern_ref[...] = jnp.zeros_like(dkern_ref)
        dgain_ref[...] = jnp.zeros_like(dgain_ref)
        dskip_ref[...] = jnp.zeros_like(dskip_ref)
        dhead_ref[...] = jnp.zeros_like(dhead_ref)

    marks = marks_ref[...]
    same = [jnp.broadcast_to(marks[:, j : j + 1], (CHUNK, LANES)) for j in range(CONV - 1)]
    ahead = [jnp.broadcast_to(marks[:, 3 + j : 4 + j], (CHUNK, LANES)) for j in range(CONV - 1)]

    def lanes(slab):
        return slice(slab * LANES, (slab + 1) * LANES)

    def window(slab):
        cols = conv_cols(slabs, slab)
        here = proj_ref[:, cols].astype(F32)
        return here, jnp.concatenate([before_ref[8:16, cols].astype(F32), here], axis=0)

    def own(slab):
        return lanes(slab - base if slab < slabs else slab - slabs + half)

    for slab in [base + j for j in range(half)] + [slabs, slabs + 1]:
        cols = lanes(slab)
        here, full = window(slab)
        total = bias_ref[0:1, cols] + kern_ref[CONV - 1 : CONV, cols] * here
        for j in range(1, CONV):
            total = total + kern_ref[CONV - 1 - j : CONV - j, cols] * (same[j - 1] * shifted_rows(full, j, False))
        gate = sigmoid(total)
        conv_ref[:, own(slab)] = total * gate
        if second or slab < slabs:
            slope_ref[:, own(slab)] = gate * (1.0 + total * (1.0 - gate))

    shifted, sizes, rate, log_decay, totals, entering, leaving = head_state(step_ref, dtb_ref, rate_ref, marks)
    wide_ref[...] = spread([sizes, leaving, entering], expand_ref[:, base * LANES : (base + half) * LANES])
    b_values = conv_ref[:, own(slabs)]
    c_values = conv_ref[:, own(slabs + 1)]
    b_low = b_values.astype(BF16)
    c_low = c_values.astype(BF16)
    c_turned = c_values.T.astype(BF16)
    shape = (CHUNK, CHUNK)
    together = (marks[:, 8:9] == row_ref[0]) & (iota(shape, 0) <= iota(shape, 1))
    mixing = jnp.where(together, dot_nt(b_low, c_low), 0.0)
    totals_row = totals.T
    low_lane = iota((CHUNK, LANES), 1) < HDIM

    if second:
        scale = part_ref[:, 3 * LANES : 3 * LANES + 1]
        pull = part_ref[:, 3 * LANES + 1 : 3 * LANES + 2]
        d_mixing = part_ref[:, 0:LANES]
        d_b = part_ref[:, LANES : 2 * LANES]
        d_c = part_ref[:, 2 * LANES : 3 * LANES]
    else:
        squares = jnp.zeros((CHUNK, LANES), F32)
        crossed = jnp.zeros((CHUNK, LANES), F32)
        for slab in range(slabs):
            cols = lanes(slab)
            gate = proj_ref[:, gate_cols(slabs, slab)].astype(F32)
            gated = scan_ref[:, cols] * (gate * sigmoid(gate))
            squares = squares + gated * gated
            crossed = crossed + gated * (gain_ref[0:1, cols] * e_ref[:, cols].astype(F32))
        scale = lax.rsqrt(jnp.sum(squares, axis=1, keepdims=True) / inner + EPS)
        pull = scale * scale * scale * (jnp.sum(crossed, axis=1, keepdims=True) / inner)
        d_mixing = jnp.zeros(shape, F32)
        d_b = jnp.zeros(shape, F32)
        d_c = jnp.zeros(shape, F32)

    def conv_back(slab, grad):
        cols = lanes(slab)
        mine = own(slab)
        pre = grad * slope_ref[:, mine]
        here, full = window(slab)
        behind = jnp.concatenate([pre, next_ref[:, mine]], axis=0)
        next_ref[:, mine] = pre[0:8]
        back = kern_ref[CONV - 1 : CONV, cols] * pre
        dkern_ref[CONV - 1 : CONV, mine] += jnp.sum(pre * here, axis=0, keepdims=True)
        for j in range(1, CONV):
            back = back + kern_ref[CONV - 1 - j : CONV - j, cols] * (ahead[j - 1] * shifted_rows(behind, j, True))
            dkern_ref[CONV - 1 - j : CONV - j, mine] += jnp.sum(
                pre * (same[j - 1] * shifted_rows(full, j, False)), axis=0, keepdims=True
            )
        dkern_ref[CONV : CONV + 1, mine] += jnp.sum(pre, axis=0, keepdims=True)
        dproj_ref[:, half * LANES + mine.start : half * LANES + mine.stop] = back.astype(BF16)

    last_row = iota((CHUNK, LANES), 0) == CHUNK - 1
    for slab in range(base, base + half):
        cols = lanes(slab)
        mine = own(slab)
        gate = proj_ref[:, gate_cols(slabs, slab)].astype(F32)
        opened = sigmoid(gate)
        silu = gate * opened
        scanned = scan_ref[:, cols]
        error = e_ref[:, cols].astype(F32)
        gated = scanned * silu
        dgain_ref[0:1, mine] += jnp.sum(error * gated * scale, axis=0, keepdims=True)
        d_gated = scale * (gain_ref[0:1, cols] * error) - gated * pull
        dproj_ref[:, mine] = (d_gated * scanned * (opened + silu * (1.0 - opened))).astype(BF16)
        grad = d_gated * silu
        grad_low = grad.astype(BF16)
        values = conv_ref[:, mine]
        size = wide_ref[0:CHUNK, mine]
        leave = wide_ref[CHUNK : 2 * CHUNK, mine]
        enter = wide_ref[2 * CHUNK : 3 * CHUNK, mine]
        stepped = values * size
        stepped_low = stepped.astype(BF16)
        grad_halves = halves(grad, low_lane)
        decays = []
        for head in (2 * slab, 2 * slab + 1):
            gap = totals_row[head : head + 1, :] - totals[:, head : head + 1]
            decays.append(jnp.exp(jnp.minimum(gap, 0.0)))
        both = jnp.concatenate([decay * mixing for decay in decays], axis=1).astype(BF16)
        ds_next = ds_ref[:, mine]
        ds_low = ds_next.astype(BF16)
        left = dot_nn(b_low, ds_low) * leave
        d_stepped = dot_nn(both, grad_halves) + left
        d_both = dot_nt(stepped_low, grad_halves)
        d_mixing = d_mixing + decays[0] * d_both[:, :CHUNK] + decays[1] * d_both[:, CHUNK:]
        entered = (grad * enter).astype(BF16)
        start = start_ref[0, :, cols]
        d_c = d_c + dot_nt(entered, start)
        d_b = d_b + dot_nt((stepped * leave).astype(BF16), ds_low)
        kept = enter[CHUNK - 1 :, :]
        ds_ref[:, mine] = ds_next * kept + dot_nn(c_turned, entered)
        skip = skip_ref[0:1, cols]
        grad_round = grad_low.astype(F32)
        step_round = stepped_low.astype(F32)
        tail = jnp.sum(step_round * left, axis=0, keepdims=True) + kept * jnp.sum(
            ds_next * start.astype(F32), axis=0, keepdims=True
        )
        steered = grad_round * (scanned - skip * values) - step_round * d_stepped
        steered = steered + jnp.where(last_row, tail, 0.0)
        sized = values * d_stepped
        for at, piece in ((0, steered), (1, sized)):
            high, low = split_low(piece)
            sums_ref[at * CHUNK : (at + 1) * CHUNK, mine] = high
            sums_ref[(at + 2) * CHUNK : (at + 3) * CHUNK, mine] = low
        dskip_ref[0:1, mine] += jnp.sum(grad * values, axis=0, keepdims=True)
        conv_back(slab, size * d_stepped + skip * grad)

    heads = dot_nn(sums_ref[...], gather_ref[base * LANES : (base + half) * LANES, :])
    heads = heads[0 : 2 * CHUNK] + heads[2 * CHUNK :]
    upper = (iota(shape, 0) <= iota(shape, 1)).astype(F32)
    d_decay = dot_nn(upper, heads[0:CHUNK], HIGH)
    d_sizes = heads[CHUNK:] + d_decay * rate
    d_step = d_sizes * sigmoid(shifted)
    dhead_ref[0:1, :] += jnp.sum(d_decay * log_decay, axis=0, keepdims=True)
    dhead_ref[1:2, :] += jnp.sum(d_step, axis=0, keepdims=True)
    if second:
        d_mixing = jnp.where(together, d_mixing, 0.0)
        d_b = d_b + dot_nn(d_mixing.astype(BF16), c_low)
        d_c = d_c + dot_nn(d_mixing.T.astype(BF16), b_low)
        dproj_ref[:, inner + 2 * LANES :] = (d_step + part_ref[:, 4 * LANES :]).astype(BF16)
        conv_back(slabs, d_b)
        conv_back(slabs + 1, d_c)
    else:
        part_ref[:, 0:LANES] = d_mixing
        part_ref[:, LANES : 2 * LANES] = d_b
        part_ref[:, 2 * LANES : 3 * LANES] = d_c
        part_ref[:, 4 * LANES :] = d_step
        part_ref[:, 3 * LANES : 3 * LANES + 1] = scale
        part_ref[:, 3 * LANES + 1 : 3 * LANES + 2] = pull


def mixer_bwd(second, deps, error, projected, step_raw, marks, rows, scanned, starts, kern, bias, rate, dtb, skip, gain, expand, gather, part=None):
    length, wide = projected.shape
    inner = gain.shape[1]
    chunks = length // CHUNK
    shape = jax.ShapeDtypeStruct

    def tokens(width):
        return pl.BlockSpec((CHUNK, width), lambda i: (chunks - 1 - i, 0))

    def whole(array):
        return pl.BlockSpec(array.shape, lambda i: (0,) * len(array.shape))

    per = CHUNK // 16
    conv = inner // 2 + (2 * LANES if second else 0)
    made = inner + (inner // 2 + conv + LANES if second else 0)
    kept = inner // 2 + 2 * LANES
    sums = (
        shape((8, conv), F32),
        shape((8, inner // 2), F32),
        shape((8, inner // 2), F32),
        shape((8, LANES), F32),
    )
    part_shape = () if second else (shape((length, 5 * LANES), F32),)
    return pl.pallas_call(
        partial(mixer_bwd_kernel, inner, second, len(deps)),
        grid=(chunks,),
        in_specs=[pl.BlockSpec(memory_space=pl.ANY) for _ in deps]
        + [
            tokens(inner),
            tokens(wide),
            pl.BlockSpec((16, wide), lambda i: (jnp.maximum((chunks - 1 - i) * per - 1, 0), 0)),
            tokens(LANES),
            tokens(LANES),
            pl.BlockSpec((1, 1, CHUNK), lambda i: (chunks - 1 - i, 0, 0)),
            tokens(inner),
            pl.BlockSpec((1, LANES, inner), lambda i: (chunks - 1 - i, 0, 0)),
        ]
        + [whole(item) for item in (kern, bias, rate, dtb, skip, gain, expand, gather)]
        + ([tokens(5 * LANES), tokens(inner)] if second else []),
        out_specs=(tokens(made),)
        + tuple(whole(item) for item in sums)
        + (() if second else (tokens(5 * LANES),)),
        out_shape=(shape((length, made), BF16),) + sums + part_shape,
        scratch_shapes=[
            pltpu.VMEM((CHUNK, kept), F32),
            pltpu.VMEM((CHUNK, kept), F32),
            pltpu.VMEM((LANES, inner // 2), F32),
            pltpu.VMEM((3 * CHUNK, inner // 2), F32),
            pltpu.VMEM((4 * CHUNK, inner // 2), BF16),
            pltpu.VMEM((8, kept), F32),
        ],
        compiler_params=pltpu.CompilerParams(vmem_limit_bytes=48 << 20),
        cost_estimate=pl.CostEstimate(flops=30 * 10**9, bytes_accessed=20 << 20, transcendentals=5 * 10**6),
        name="mixer_bwd_second" if second else "mixer_bwd_first",
    )(*deps, error, projected, projected, step_raw, marks, rows, scanned, starts, kern, bias, rate, dtb, skip, gain, expand, gather,
      *(part or ()))


def norm_scale(values):
    return lax.rsqrt(jnp.mean(values * values, axis=-1, keepdims=True) + EPS)


def norm_back(values, scale, gain, error):
    pulled = gain * error
    pull = jnp.mean(values * pulled, axis=-1, keepdims=True)
    grad = scale * pulled - values * (scale * scale * scale * pull)
    return grad, jnp.sum(error * (values * scale), axis=0)


def rotary_tables(length, width):
    half = width // 2
    place = (iota((length, LANES), 1) % half).astype(F32)
    freq = jnp.exp(-(place * (2.0 / width)) * math.log(THETA))
    angle = iota((length, LANES), 0).astype(F32) * freq
    return jnp.cos(angle), jnp.sin(angle)


def places(axis, bit):
    return [(i, i ^ bit) for i in range(lax.axis_size(axis))]


def turns(axis, by):
    size = lax.axis_size(axis)
    return [(i, (i + by) % size) for i in range(size)]


def rep_bits():
    count = lax.axis_size("rep").bit_length() - 1
    return [1 << i for i in range(count)]


def bit_orders(bits):
    rest = bits[1:]
    return rest + bits[:1], rest[::-1] + bits[:1]


def have(bit):
    return (lax.axis_index("rep") & bit) != 0


def my_place(bits):
    place = jnp.int32(0)
    for bit in bits:
        place = place * 2 + have(bit).astype(jnp.int32)
    return place


def nothing(*refs):
    pass


def after(value, *deps):
    if not deps:
        return value
    return pl.pallas_call(
        nothing,
        in_specs=[pl.BlockSpec(memory_space=pl.ANY)] * (1 + len(deps)),
        out_specs=pl.BlockSpec(memory_space=pl.ANY),
        out_shape=jax.ShapeDtypeStruct(value.shape, value.dtype),
        input_output_aliases={0: 0},
        name="after",
    )(value, *deps)


class Moves:
    def start(self, stages):
        self.stages = list(stages)
        self.under_way = None
        self.flying = []

    def advance(self, *deps):
        if self.under_way is not None:
            self.under_way([after(item, *deps) for item in self.flying])
            self.under_way = None
        if self.stages:
            self.flying, self.under_way = self.stages.pop(0)()
        return self

    def finish(self):
        while self.stages or self.under_way is not None:
            self.advance()

    def swap(self, bit, place):
        def send():
            return [
                lax.ppermute(part, "rep", places("rep", own)) for part, own in zip(self.parts, bit)
            ], take

        def take(others):
            parts = []
            for part, other, own in zip(self.parts, others, bit):
                mine = have(own)
                low, high = jnp.where(mine, other, part), jnp.where(mine, part, other)
                parts.append(jnp.concatenate([low, high], axis=place + self.bits.index(own)))
            self.parts = parts

        return send

    def fold(self, bit, place):
        def send():
            return [
                lax.ppermute(side(part, place + self.bits.index(own), own, False), "rep", places("rep", own))
                for part, own in zip(self.parts, bit)
            ], take

        def take(others):
            self.parts = [
                folded(part, other, place + self.bits.index(own), own)
                for part, other, own in zip(self.parts, others, bit)
            ]

        return send


def side(part, axis, bit, mine):
    at = have(bit).astype(jnp.int32)
    return lax.dynamic_slice_in_dim(part, at if mine else 1 - at, 1, axis=axis)


def folded(part, other, axis, bit):
    return (side(part, axis, bit, True).astype(F32) + other.astype(F32)).astype(BF16)


class Gather(Moves):
    def __init__(self, weight):
        self.bits = rep_bits()
        self.groups = lax.axis_size("shard")
        self.shape = (self.groups * weight.shape[0], weight.shape[1])
        self.weight = weight
        self.start([self.over_shard] + [self.swap(bit, 1) for bit in zip(*bit_orders(self.bits))])

    def send_after(self, *deps):
        self.deps = deps
        return self.advance()

    def over_shard(self):
        rows, columns = self.weight.shape[0] >> len(self.bits), self.weight.shape[1]
        mine = lax.dynamic_slice_in_dim(self.weight, my_place(self.bits) * rows, rows, 0)
        mine = after(mine, *self.deps)
        here = lax.axis_index("shard")

        def take(others):
            parts = jnp.zeros((self.groups, rows, columns), self.weight.dtype)
            parts = lax.dynamic_update_slice(parts, mine[None], (here, 0, 0))
            for by, other in enumerate(others, 1):
                parts = lax.dynamic_update_slice(parts, other[None], ((here - by) % self.groups, 0, 0))
            parts = parts.reshape((self.groups,) + (1,) * len(self.bits) + (rows, columns))
            half = self.groups // 2
            self.parts = [parts[:half], parts[half:]] if half else [parts]

        return [lax.ppermute(mine, "shard", turns("shard", by)) for by in range(1, self.groups)], take

    def result(self):
        self.finish()
        return jnp.concatenate(self.parts, axis=0).reshape(self.shape)


def pair_hop(part, axis, bit):
    return lax.ppermute(side(part, axis, bit, False), "rep", places("rep", bit))


def by_place(grad):
    bits = rep_bits()
    groups = lax.axis_size("shard")
    rows, columns = grad.shape[0] // groups >> len(bits), grad.shape[1]
    return grad.reshape((groups,) + (2,) * len(bits) + (rows, columns))


def early_hop(grad):
    bits = rep_bits()
    return [pair_hop(by_place(grad), len(bits), bits[0])] if bits else []


class Sum(Moves):
    def __init__(self, *grads, early=()):
        bits = rep_bits()
        self.bits = bits[::-1]
        self.early = early
        self.groups = lax.axis_size("shard")
        self.rows = grads[0].shape[0] // self.groups >> len(bits)
        self.widths = [grad.shape[1] for grad in grads]
        self.columns = sum(self.widths)
        self.grads = [by_place(grad) for grad in grads]
        orders = list(zip(*bit_orders(bits)))
        self.start([self.over_bit_0] + [self.fold(bit, 1) for bit in orders[:-1]] + [self.over_shard])
        self.advance()

    def over_bit_0(self):
        axis = len(self.bits)

        def take(others):
            parts = self.grads
            if self.bits:
                parts = [folded(part, other, axis, self.bits[-1]) for part, other in zip(parts, others)]
            part = jnp.concatenate(parts, axis=-1)
            half = self.groups // 2
            self.parts = [part[:half], part[half:]] if half else [part]

        if not self.bits:
            return [], take
        late = self.grads[len(self.early) :]
        return list(self.early) + [pair_hop(part, axis, self.bits[-1]) for part in late], take

    def over_shard(self):
        part = jnp.concatenate(self.parts, axis=0).reshape(self.groups, self.rows, self.columns)
        here = lax.axis_index("shard")

        def of(by):
            return lax.dynamic_index_in_dim(part, (here + by) % self.groups, 0, keepdims=False)

        def take(others):
            total = of(0).astype(F32)
            for other in others:
                total = total + other.astype(F32)
            self.parts = [total.astype(BF16)]

        return [lax.ppermute(of(by), "shard", turns("shard", by)) for by in range(1, self.groups)], take

    def gather(self, *deps):
        self.finish()
        self.whole = lax.all_gather(after(self.parts[0], *deps), "rep", axis=0, tiled=True)
        return self.whole

    def result(self):
        whole = self.whole.astype(F32)
        ends = [sum(self.widths[: at + 1]) for at in range(len(self.widths))]
        return [whole[:, end - width : end] for end, width in zip(ends, self.widths)]


def gathered(weight):
    parts = lax.axis_size("rep")
    rows = weight.shape[0] // parts
    mine = lax.dynamic_slice_in_dim(weight, lax.axis_index("rep") * rows, rows, 0)
    return lax.all_gather(mine, ("shard", "rep"), axis=0, tiled=True)


def summed_small(values):
    for axis in ("rep", "shard"):
        bit = 1
        while bit < lax.axis_size(axis):
            values = values + lax.ppermute(values, axis, places(axis, bit))
            bit *= 2
    return values


def shards(
    x_in,
    segment_ids,
    norm_in,
    mix_in,
    attn_in,
    attn_out,
    mix_out,
    norm_ff,
    ff_in,
    ff_out,
    conv_kernel,
    conv_bias,
    log_rate,
    dt_bias,
    skip,
    gate_norm,
    cotangent,
):
    _, length, model = x_in.shape
    inner = gate_norm.shape[0]
    channels = conv_bias.shape[0]
    heads = log_rate.shape[0]
    qkv = attn_in.shape[1]
    lane_pad = LANES - heads

    main = inner + channels
    half = inner // 2
    extra = jnp.concatenate([attn_in, jnp.stack([norm_in, norm_ff], axis=1)], axis=1)
    from_small = Gather(jnp.pad(extra, ((0, 0), (0, LANES - 2)))).send_after()
    from_main = Gather(
        jnp.concatenate(
            [
                mix_in[:, :half],
                mix_in[:, inner : inner + half],
                mix_in[:, half:inner],
                mix_in[:, inner + half :],
                jnp.zeros((mix_in.shape[0], lane_pad), BF16),
            ],
            axis=1,
        )
    ).send_after(*from_small.flying)
    small_in = from_small.result()
    main_in = from_main.result()
    outs_wide = attn_out.shape[1] + mix_out.shape[1]
    ff_wide = outs_wide + ff_in.shape[1]
    late = gathered(jnp.concatenate([attn_out, mix_out, ff_in, ff_out], axis=1))
    full_outs = late[:, :outs_wide]
    full_ff_in = late[:, outs_wide:ff_wide]
    full_ff_out = late[:, ff_wide:]

    ids = segment_ids.reshape(length)
    marks = token_marks(ids)
    id_row = ids.astype(F32).reshape(1, length)
    chunk_rows = ids.astype(F32).reshape(length // CHUNK, 1, CHUNK)
    cosine, sine = rotary_tables(length, HDIM)

    def row(values, pad=0):
        return jnp.pad(values.astype(F32).reshape(1, -1), ((0, 7), (0, pad)))

    kern = jnp.pad(conv_kernel.astype(F32), ((0, 4), (0, 0)))
    bias = row(conv_bias)
    rate = row(log_rate, lane_pad)
    dtb = row(dt_bias, lane_pad)
    skips = row(jnp.repeat(skip, inner // heads))
    gain = row(gate_norm)
    owner = jnp.arange(inner, dtype=jnp.int32) // (inner // heads)
    expand = (owner[None, :] == jnp.arange(LANES, dtype=jnp.int32)[:, None]).astype(BF16)
    gather = expand.T
    expand = jnp.concatenate([expand, expand], axis=0)

    resid = x_in.reshape(length, model).astype(F32)
    full_norms = small_in[:, qkv : qkv + 2].astype(F32).T
    first_scale = norm_scale(resid)
    first_low = (resid * first_scale * full_norms[0]).astype(BF16)
    attn_proj = dot_nn(first_low, small_in[:, :qkv])
    query, keys, values, attended, lse = attention_fwd(attn_proj, cosine, sine, marks, id_row)
    step_raw = dot_nn(first_low, main_in[:, main:])
    projected = dot_nn(first_low, main_in[:, :main]).astype(BF16)
    scanned, starts, mixed = mixer_fwd(
        projected, step_raw, marks, chunk_rows, kern, bias, rate, dtb, skips, gain, expand
    )
    attw = attended.shape[1]
    branches = jnp.concatenate([attended, mixed], axis=1)
    hidden = resid + dot_nt(branches, full_outs)
    second_scale = norm_scale(hidden)
    second_low = (hidden * second_scale * full_norms[1]).astype(BF16)
    ff_proj = dot_nn(second_low, full_ff_in)
    width = ff_proj.shape[1] // 2
    opened = sigmoid(ff_proj[:, :width])
    silu = ff_proj[:, :width] * opened
    up = ff_proj[:, width:]
    act_low = (silu * up).astype(BF16)
    output = (hidden + dot_nt(act_low, full_ff_out)).astype(BF16).reshape(x_in.shape)

    grad_out = cotangent.reshape(length, model)
    ff_out_part = dot_tn(grad_out, act_low).astype(BF16)
    grad_act = dot_nn(grad_out, full_ff_out)
    grad_ff = jnp.concatenate(
        [grad_act * up * (opened + silu * (1.0 - opened)), grad_act * silu], axis=1
    ).astype(BF16)
    sum_ff = Sum(ff_out_part, dot_tn(second_low, grad_ff).astype(BF16))
    grad_second = dot_nt(grad_ff, full_ff_in)
    grad_hidden, norm_ff_grad = norm_back(hidden, second_scale, full_norms[1], grad_second)
    grad_hidden = grad_hidden + grad_out.astype(F32)
    branch_low = grad_hidden.astype(BF16)
    sum_ff.advance(branch_low)
    outs_part = dot_tn(branch_low, branches).astype(BF16)
    grad_branches = dot_nn(branch_low, full_outs).astype(BF16)
    d_attn = attention_bwd(
        sum_ff.parts, query, keys, values, lse, grad_branches[:, :attw], cosine, sine, marks, id_row
    )
    sum_ff.advance(d_attn)
    sum_mid = Sum(outs_part, dot_tn(first_low, d_attn).astype(BF16))
    common = (step_raw, marks, chunk_rows, scanned, starts, kern, bias, rate, dtb, skips, gain, expand, gather)
    d_first, d_kern_a, d_gain_a, d_skip_a, d_head_a, handed = mixer_bwd(
        False, sum_ff.parts, grad_branches[:, attw:], projected, *common
    )
    sum_ff.advance(d_first)
    sum_mid.advance(d_first)
    first_part = dot_tn(first_low, d_first).astype(BF16)
    first_hop = early_hop(first_part)
    d_main, d_kern_b, d_gain_b, d_skip_b, d_head_b = mixer_bwd(
        True, sum_ff.parts + sum_mid.parts, grad_branches[:, attw:], projected, *common, part=(handed, d_first)
    )
    sum_ff.advance(d_main)
    sum_mid.advance(d_main)
    second_part = dot_tn(first_low, d_main[:, inner:]).astype(BF16)
    sum_main = Sum(first_part, second_part, early=[after(item, d_main) for item in first_hop])
    sum_main.advance()
    grad_first = dot_nt(d_main, main_in) + dot_nt(d_attn, small_in[:, :qkv])
    grad_resid, norm_in_grad = norm_back(resid, first_scale, full_norms[0], grad_first)
    input_grad = (grad_resid + grad_hidden).astype(BF16).reshape(x_in.shape)
    while sum_main.stages:
        landing = tuple(sum_main.flying)
        sum_main.advance()
        sum_mid.advance(*landing)
        sum_ff.advance(*landing)
    sum_main.gather(sum_mid.gather(sum_ff.gather()))
    ff_out_grad, ff_in_grad = sum_ff.result()
    outs_sum, attn_in_grad = sum_mid.result()
    main_sum = jnp.concatenate(sum_main.result(), axis=1)
    mix_in_grad = jnp.concatenate(
        [
            main_sum[:, :half],
            main_sum[:, inner : inner + half],
            main_sum[:, half:inner],
            main_sum[:, inner + half : main + heads],
        ],
        axis=1,
    )
    d_kern = jnp.concatenate([d_kern_a, d_kern_b], axis=1)
    d_gain = jnp.concatenate([d_gain_a, d_gain_b], axis=1)
    d_skip = jnp.concatenate([d_skip_a, d_skip_b], axis=1)
    d_head = d_head_a + d_head_b

    pieces = (
        d_kern[:CONV].reshape(-1),
        d_kern[CONV],
        d_gain[0],
        jnp.sum(d_skip[0].reshape(heads, -1), axis=1),
        d_head[0, :heads],
        d_head[1, :heads],
        norm_in_grad,
        norm_ff_grad,
    )
    packed = summed_small(jnp.concatenate(pieces))
    split = []
    at = 0
    for piece in pieces:
        split.append(packed[at : at + piece.shape[0]])
        at += piece.shape[0]
    rows = norm_in.shape[0]
    mine = lax.axis_index("shard") * rows
    return (
        output,
        input_grad,
        lax.dynamic_slice_in_dim(split[6], mine, rows, 0),
        mix_in_grad,
        attn_in_grad,
        outs_sum[:, :attw],
        outs_sum[:, attw:],
        lax.dynamic_slice_in_dim(split[7], mine, rows, 0),
        ff_in_grad,
        ff_out_grad,
        split[0].reshape(conv_kernel.shape),
        split[1],
        split[4],
        split[5],
        split[3],
        split[2],
    )


def solution(mesh):
    in_specs = (
        P(("rep", "shard"), None, None),
        P(("rep", "shard"), None),
        P("shard"),
        P("shard", None),
        P("shard", None),
        P("shard", None),
        P("shard", None),
        P("shard"),
        P("shard", None),
        P("shard", None),
        P(),
        P(),
        P(),
        P(),
        P(),
        P(),
        P(("rep", "shard"), None, None),
    )
    out_specs = (
        P(("rep", "shard"), None, None),
        P(("rep", "shard"), None, None),
        P("shard"),
        P("shard", None),
        P("shard", None),
        P("shard", None),
        P("shard", None),
        P("shard"),
        P("shard", None),
        P("shard", None),
        P(),
        P(),
        P(),
        P(),
        P(),
        P(),
    )
    return jax.shard_map(shards, mesh=mesh, in_specs=in_specs, out_specs=out_specs, check_vma=False)
```
